32 devices in a mesh: pole: 2 (over y), row: 4 (over z), col: 4 (over x, core).
Axes of the slice: x: 2, y: 2, z: 4, core: 2. Of those that a mesh axis runs over, the one named last changes fastest.
Arguments:
- inverse_root: float32 [2048, 1024], P(('pole', 'row'), 'col'), parts along dimension 0, may hold values from -6 to 6, as said below
- lower_first: float32 [2048, 512], P(('pole', 'col'), 'row'), parts along dimension 0, may hold values from -0.1875 to 0.1875
- mask_first: int32 [8, 4], P('col', 'row'), may hold values 0 or 1
- dinv_first: float32 [256, 512], P('pole', 'col'), parts along dimension 0, may hold values from -6 to 6
- lower_second: float32 [2048, 512], P(('pole', 'col'), 'row'), parts along dimension 0, may hold values from -0.1875 to 0.1875
- mask_second: int32 [8, 4], P('col', 'row'), may hold values 0 or 1
- parent: int32 [4], replicated, may hold values from 0 to 3
- lower_parent: float32 [256, 512], P('pole', 'col'), parts along dimension 0, may hold values from -0.5 to 0.5
- dinv_second: float32 [256, 512], P('pole', 'col'), parts along dimension 0, may hold values from -6 to 6
Outputs:
- inverse_first: float32 [2048, 512], P(('pole', 'row'), 'col'), parts along dimension 0
- diag_first: float32 [256, 512], P('pole', 'col'), parts along dimension 0
- inverse_second: float32 [2048, 512], P(('pole', 'row'), 'col'), parts along dimension 0
- diag_second: float32 [256, 512], P('pole', 'col'), parts along dimension 0
The draws below stay inside these ranges and needn't reach their ends.
There are 2 independent parts, one for each index of `pole`. The reference program is written for one: setup_inputs(seed, part) draws one part's arguments, and reference() takes and returns one part's arrays. A program takes and returns all parts, laid end to end along the dimension named above; an argument that names none is the same for every part. Nothing has to cross between parts.
Inputs may be any that keep to these rules, and one draw needn't show every extreme that they name: `inverse_root`: symmetric.
All inputs are finite; a program needn't handle non-finite values. No bound on the sum of `mask_first` or of `mask_second` on one device may be relied on, other than what follows from the above.
Results may differ from the reference program's by a relative error of at most 0.000071.
Values sent between devices are 32-bit elements; how exact they have to be, the bound alone decides.
No kernel may reach another device: no remote copies, remote signals or barrier semaphores. Data moves between devices by JAX's collectives and lax.ppermute only.
A program may use at most 64 MiB of HBM per device.

```python
import jax
import jax.numpy as jnp
from jax import lax

BLOCK = 128
ROOT_BLOCKS = 8
FIRST_BLOCKS = 4
SECOND_BLOCKS = 4
ROOT = 1024
FIRST = 512
SECOND = 512


def draw_inverse_root(key, part):
    key = jax.random.fold_in(key, 11)
    sample = jax.random.normal(key, (ROOT, ROOT), jnp.float32)
    return jnp.clip((sample + sample.T) * 0.7071, -6.0, 6.0)


def draw_parent(key, part):
    key = jax.random.fold_in(key, 23)
    count = FIRST_BLOCKS
    popular = jax.random.randint(jax.random.fold_in(key, 1), (), 0, count, jnp.int32)
    spread = jax.random.randint(jax.random.fold_in(key, 2), (SECOND_BLOCKS,), 0, count, jnp.int32)
    pick = jax.random.randint(jax.random.fold_in(key, 3), (SECOND_BLOCKS,), 0, 2, jnp.int32)
    values = jnp.where(pick == 0, popular, spread)
    start = jax.random.randint(jax.random.fold_in(key, 4), (), 0, SECOND_BLOCKS, jnp.int32)
    values = values.at[start % SECOND_BLOCKS].set((start + count - 1) % count)
    values = values.at[(start + 1) % SECOND_BLOCKS].set((start + 1 + count // 2) % count)
    values = values.at[(start + 2) % SECOND_BLOCKS].set(count - 1)
    values = values.at[(start + 3) % SECOND_BLOCKS].set(0)
    return values.astype(jnp.int32)


def plant(values, key, smallest, high):
    dims = values.shape
    spot = [jax.random.randint(jax.random.fold_in(key, axis), (), 0, dims[axis]) for axis in range(len(dims))]
    values = values.at[tuple(spot)].set(smallest)
    longest = dims.index(max(dims))
    spot[longest] = (spot[longest] + 1) % dims[longest]
    return values.at[tuple(spot)].set(high)


def steps_of(stream_key, dims, shards, low, high):
    def one(dim, blocks):
        heights = jax.random.uniform(jax.random.fold_in(jax.random.fold_in(stream_key, 6), dim), (blocks,), jnp.float32, low / len(shards), high / len(shards))
        return jnp.repeat(jnp.exp(heights), dims[dim] // blocks).reshape((-1,) + (1,) * (len(dims) - dim - 1))

    loudness = one(*shards[0])
    for cut in shards[1:]:
        loudness = loudness * one(*cut)
    return loudness


def noise(own_key, dims, scale, limit, split=(), held_as=jnp.bfloat16):
    factor_of = steps_of(own_key, dims, split, -0.22, 0.18) if split else 1.0
    values = jax.random.normal(own_key, dims, jnp.float32) * scale * factor_of
    return jnp.minimum(jnp.maximum(values, -limit), limit).astype(held_as)


def setup_inputs(seed: int = 0, part: int = 0) -> dict:
    streams_of = jax.random.split(jax.random.key(seed), 10)
    part_keys = jax.random.split(jax.random.fold_in(streams_of[9], part), 10)
    return {
        "inverse_root": draw_inverse_root(jax.random.fold_in(jax.random.fold_in(streams_of[9], part), 71), part),
        "lower_first": noise(part_keys[1], (ROOT, FIRST), ROOT ** -0.5, 0.1875, ((0, 4), (1, 4)), jnp.float32),
        "mask_first": plant((jax.random.randint(streams_of[2], (ROOT_BLOCKS, FIRST_BLOCKS), 0, 2) < 1).astype(jnp.int32), jax.random.fold_in(streams_of[2], 1), 0, 1),
        "dinv_first": noise(part_keys[3], (BLOCK, FIRST), 1.0, 6.0, ((1, 4),), jnp.float32),
        "lower_second": noise(part_keys[4], (ROOT, SECOND), ROOT ** -0.5, 0.1875, ((0, 4), (1, 4)), jnp.float32),
        "mask_second": plant((jax.random.randint(streams_of[5], (ROOT_BLOCKS, SECOND_BLOCKS), 0, 2) < 1).astype(jnp.int32), jax.random.fold_in(streams_of[5], 1), 0, 1),
        "parent": draw_parent(jax.random.fold_in(streams_of[9], 71), part),
        "lower_parent": noise(part_keys[7], (BLOCK, SECOND), BLOCK ** -0.5, 0.5, ((1, 4),), jnp.float32),
        "dinv_second": noise(part_keys[8], (BLOCK, SECOND), 1.0, 6.0, ((1, 4),), jnp.float32),
    }


highest = lax.Precision.HIGHEST


def masked_blocks(values, pattern):
    rows_blocks = pattern.shape[0]
    cols_blocks = pattern.shape[1]
    grid = values.reshape(rows_blocks, values.shape[0] // rows_blocks, cols_blocks, values.shape[1] // cols_blocks)
    return (grid * pattern.astype(jnp.float32)[:, None, :, None]).reshape(values.shape)


def diag_blocks(left, right, block_size):
    count = left.shape[1] // block_size
    left_cube = left.reshape(left.shape[0], count, block_size)
    right_cube = right.reshape(right.shape[0], count, block_size)
    result = jnp.einsum('rkb,rkc->bkc', left_cube, right_cube, precision=highest)
    return result.reshape(block_size, count * block_size)


def parent_terms(values, diagonal, lower_blocks, parent_ids, first_ids):
    block_size = lower_blocks.shape[0]
    second_count = parent_ids.shape[0]
    first_count = first_ids.shape[0]
    selector = (parent_ids[:, None] == first_ids[None, :]).astype(jnp.float32)
    lower_cube = lower_blocks.reshape(block_size, second_count, block_size)
    weights = jnp.einsum('kj,bkc->jbkc', selector, lower_cube, precision=highest)
    weights = weights.reshape(first_count * block_size, second_count * block_size)
    coupling = jnp.dot(values, weights, precision=highest, preferred_element_type=jnp.float32)
    diag_cube = diagonal.reshape(block_size, first_count, block_size)
    chosen = jnp.einsum('kj,bji->kbi', selector, diag_cube, precision=highest)
    product = jnp.einsum('kbi,ikc->bkc', chosen, lower_cube, precision=highest)
    return coupling, product.reshape(block_size, second_count * block_size)


def reference(inverse_root, lower_first, mask_first, dinv_first, lower_second, mask_second, parent, lower_parent, dinv_second):
    first = masked_blocks(lower_first, mask_first)
    inverse_first = -jnp.dot(inverse_root, first, precision=highest, preferred_element_type=jnp.float32)
    diag_first = dinv_first - diag_blocks(first, inverse_first, BLOCK)
    second = masked_blocks(lower_second, mask_second)
    first_ids = jnp.arange(FIRST_BLOCKS, dtype=jnp.int32)
    coupling, product = parent_terms(inverse_first, diag_first, lower_parent, parent.astype(jnp.int32), first_ids)
    inverse_second = -(jnp.dot(inverse_root, second, precision=highest, preferred_element_type=jnp.float32) + coupling)
    diag_second = dinv_second - diag_blocks(second, inverse_second, BLOCK) + diag_blocks(coupling, second, BLOCK) + diag_blocks(lower_parent, product, BLOCK)
    return (inverse_first, diag_first, inverse_second, diag_second)
```

```python
import functools

import jax
import jax.numpy as jnp
from jax import lax
from jax.experimental import pallas as pl
from jax.experimental.pallas import tpu as pltpu
from jax.sharding import PartitionSpec as P

VMEM = pl.BlockSpec(memory_space=pltpu.VMEM)
SMEM = pl.BlockSpec(memory_space=pltpu.SMEM)
NN = ((1,), (0,))
TN = ((0,), (0,))


def split(x):
    high = x.astype(jnp.bfloat16)
    return high, (x - high.astype(jnp.float32)).astype(jnp.bfloat16)


def dot_split(a, b, dims):
    def one(left, right):
        return lax.dot_general(left, right, (dims, ((), ())), preferred_element_type=jnp.float32)

    return one(a[0], b[0]) + (one(a[0], b[1]) + one(a[1], b[0]))


def dot3(a, b, dims=NN):
    return dot_split(split(a), split(b), dims)


def slots(nrow, ncol):
    q = ncol // nrow
    r, c = lax.axis_index("row"), lax.axis_index("col")
    own = [(r * q + i) ^ c for i in range(q)]
    return (r * q + c % q) ^ c, own, c


def first_kernel(nrow, ncol, *refs):
    r_refs, f_refs = refs[:ncol], refs[ncol : 2 * ncol]
    dinv_ref, x_ref, z_ref, rh_ref, rl_ref, fh_ref, fl_ref = refs[2 * ncol :]
    base, own, _ = slots(nrow, ncol)
    depth = f_refs[0].shape[0]
    for t in range(ncol):
        slot = base ^ t
        fh_ref[slot], fl_ref[slot] = split(f_refs[t][...])
    total = None
    for j in range(ncol):
        parts = split(r_refs[j][...])
        rh_ref[j], rl_ref[j] = parts
        term = dot_split(parts, (fh_ref[j], fl_ref[j]), NN)
        total = term if total is None else total + term
    x = -total
    x_ref[...] = x
    rows = x.shape[0]
    z_ref[:rows] = x
    diag = None
    for i, slot in enumerate(own):
        term = dot_split(
            (fh_ref[slot], fl_ref[slot]), split(total[i * depth : (i + 1) * depth]), TN
        )
        diag = term if diag is None else diag + term
    block = diag.shape[0]
    z_ref[rows : rows + block] = diag
    z_ref[rows + block :] = dinv_ref[...]


def parent_kernel(nrow, ncol, *refs):
    z_refs = refs[:ncol]
    parent_ref, lower_ref, dinv_ref, c_ref, t_ref, e_ref, sel_ref = refs[ncol:]
    c = lax.axis_index("col")
    slot = parent_ref[c] ^ c
    for j in range(ncol):

        @pl.when(slot == j)
        def _(j=j):
            sel_ref[...] = z_refs[j][...]

    lower = split(lower_ref[...])
    block = lower_ref.shape[0]
    rows = c_ref.shape[0]
    product = dot_split(split(sel_ref[...]), lower, NN)
    c_ref[...] = product[:rows]
    t_ref[...] = dot_split(lower, split(product[rows : rows + block]), TN)
    e_ref[...] = dinv_ref[...] + dot_split(lower, split(product[rows + block :]), TN)


def second_kernel(nrow, ncol, *refs):
    s_refs = refs[:ncol]
    rh_ref, rl_ref, c_ref, t_ref, z_ref, y_ref, m_ref, sh_ref, sl_ref = refs[ncol:]
    base, own, _ = slots(nrow, ncol)
    depth = s_refs[0].shape[0]
    for t in range(ncol):
        slot = base ^ t
        sh_ref[slot], sl_ref[slot] = split(s_refs[t][...])
    total = c_ref[...]
    for j in range(ncol):
        total += dot_split((rh_ref[j], rl_ref[j]), (sh_ref[j], sl_ref[j]), NN)
    y_ref[...] = -total
    coupling = c_ref[...]
    diag = t_ref[...]
    for i, slot in enumerate(own):
        mine = (sh_ref[slot], sl_ref[slot])
        here = slice(i * depth, (i + 1) * depth)
        diag += dot_split(mine, split(total[here]), TN)
        diag += dot_split(split(coupling[here]), mine, TN)
    rows = c_ref.shape[0]
    block = diag.shape[0]
    across = lax.broadcasted_iota(jnp.int32, diag.shape, 1)
    down = lax.broadcasted_iota(jnp.int32, diag.shape, 0)
    m_ref[:block] = jnp.where(down <= across, z_ref[rows : rows + block], diag)
    line = jnp.sum(jnp.where(down == across, diag, 0.0), axis=0, keepdims=True)
    m_ref[block:] = jnp.broadcast_to(line, (m_ref.shape[0] - block, line.shape[1]))


def last_kernel(m_ref, dinv_ref, e_ref, one_ref, two_ref):
    block = dinv_ref.shape[0]
    m = m_ref[:block]
    across = lax.broadcasted_iota(jnp.int32, m.shape, 1)
    down = lax.broadcasted_iota(jnp.int32, m.shape, 0)
    turned = m.T
    one_ref[...] = dinv_ref[...] + jnp.where(down <= across, m, turned)
    line = jnp.broadcast_to(m_ref[block : block + 1], m.shape)
    two_ref[...] = e_ref[...] + jnp.where(
        down == across, line, jnp.where(down > across, m, turned)
    )


def call(kernel, outs, scratch, *args):
    size = 0
    for shape, dtype in [(a.shape, a.dtype) for a in args] + outs + scratch:
        if len(shape) > 1:
            count = 1
            for extent in shape:
                count *= extent
            size += count * jnp.dtype(dtype).itemsize
    limit = min(56 << 20, 3 * size + (4 << 20))
    return pl.pallas_call(
        kernel,
        out_shape=[jax.ShapeDtypeStruct(shape, dtype) for shape, dtype in outs],
        in_specs=[SMEM if a.ndim == 1 else VMEM for a in args],
        out_specs=[VMEM] * len(outs),
        scratch_shapes=[pltpu.VMEM(shape, dtype) for shape, dtype in scratch],
        compiler_params=pltpu.CompilerParams(vmem_limit_bytes=limit),
        cost_estimate=pl.CostEstimate(flops=4 * size * 64, bytes_accessed=size, transcendentals=0),
    )(*args)


def masked(values, pattern):
    rows, cols = pattern.shape
    grid = values.reshape(rows, values.shape[0] // rows, cols, values.shape[1] // cols)
    return (grid * pattern.astype(jnp.float32)[:, None, :, None]).reshape(values.shape)


def swap(x, axis, size, bit):
    return lax.ppermute(x, axis, [(i, i ^ bit) for i in range(size)])


def gather_xor(x, axis, size):
    blocks = {0: x}
    bit = size // 2
    while bit:
        for j in sorted(blocks):
            blocks[j ^ bit] = swap(blocks[j], axis, size, bit)
        bit //= 2
    return [blocks[j] for j in range(size)]


def turn(values, nrow, ncol, block):
    q = ncol // nrow
    out = []
    for t in range(ncol):
        pairs = []
        for r in range(nrow):
            for c in range(ncol):
                k = (r * q + c % q) ^ t
                pairs.append(((c // q) * ncol + k, r * ncol + c))
        part = values
        if q > 1:
            which = (lax.axis_index("col") ^ t) % q
            part = lax.dynamic_slice_in_dim(values, which * block, block, 1)
        out.append(lax.ppermute(part, ("row", "col"), pairs))
    return out


def on_device(
    nrow,
    ncol,
    inverse_root,
    lower_first,
    mask_first,
    dinv_first,
    lower_second,
    mask_second,
    parent,
    lower_parent,
    dinv_second,
):
    f32, bf16 = jnp.float32, jnp.bfloat16
    block = dinv_first.shape[0]
    rows, depth = inverse_root.shape
    first = masked(lower_first, mask_first)
    second = masked(lower_second, mask_second)
    f_parts = turn(first, nrow, ncol, block)
    r_parts = gather_xor(inverse_root, "col", ncol)
    s_parts = turn(second, nrow, ncol, block)
    halves = [((ncol, rows, depth), bf16)] * 2
    pieces = [((ncol, depth, block), bf16)] * 2
    inverse_first, z, r_high, r_low = call(
        functools.partial(first_kernel, nrow, ncol),
        [((rows, block), f32), ((rows + 2 * block, block), f32)] + halves,
        pieces,
        *r_parts,
        *f_parts,
        dinv_first,
    )
    z_parts = gather_xor(z, "col", ncol)
    coupling, parent_diag, start = call(
        functools.partial(parent_kernel, nrow, ncol),
        [((rows, block), f32), ((block, block), f32), ((block, block), f32)],
        [(z.shape, f32)],
        *z_parts,
        parent,
        lower_parent,
        dinv_second,
    )
    inverse_second, packed = call(
        functools.partial(second_kernel, nrow, ncol),
        [((rows, block), f32), ((block + 8, block), f32)],
        pieces,
        *s_parts,
        r_high,
        r_low,
        coupling,
        parent_diag,
        z,
    )
    bit = 1
    while bit < nrow:
        packed = packed + swap(packed, "row", nrow, bit)
        bit *= 2
    diag_first, diag_second = call(
        last_kernel, [((block, block), f32)] * 2, [], packed, dinv_first, start
    )
    return (inverse_first, diag_first, inverse_second, diag_second)


def solution(mesh):
    in_specs = (
        P(("pole", "row"), "col"),
        P(("pole", "col"), "row"),
        P("col", "row"),
        P("pole", "col"),
        P(("pole", "col"), "row"),
        P("col", "row"),
        P(),
        P("pole", "col"),
        P("pole", "col"),
    )
    out_specs = (
        P(("pole", "row"), "col"),
        P("pole", "col"),
        P(("pole", "row"), "col"),
        P("pole", "col"),
    )
    return jax.shard_map(
        functools.partial(on_device, mesh.shape["row"], mesh.shape["col"]),
        mesh=mesh,
        in_specs=in_specs,
        out_specs=out_specs,
        check_vma=False,
    )
```

```python
import functools

import jax
import jax.numpy as jnp
from jax import lax
from jax.experimental import pallas as pl
from jax.experimental.pallas import tpu as pltpu
from jax.sharding import PartitionSpec as P

VMEM = pl.BlockSpec(memory_space=pltpu.VMEM)
SMEM = pl.BlockSpec(memory_space=pltpu.SMEM)
NN = ((1,), (0,))
TN = ((0,), (0,))


def split(x):
    high = x.astype(jnp.bfloat16)
    return high, (x - high.astype(jnp.float32)).astype(jnp.bfloat16)


def dot_split(a, b, dims):
    def one(left, right):
        return lax.dot_general(left, right, (dims, ((), ())), preferred_element_type=jnp.float32)

    return one(a[0], b[0]) + (one(a[0], b[1]) + one(a[1], b[0]))


def dot3(a, b, dims=NN):
    return dot_split(split(a), split(b), dims)


def slots(nrow, ncol):
    q = ncol // nrow
    r, c = lax.axis_index("row"), lax.axis_index("col")
    own = [(r * q + i) ^ c for i in range(q)]
    return (r * q + c % q) ^ c, own, c


def first_kernel(nrow, ncol, *refs):
    r_refs, f_refs = refs[:ncol], refs[ncol : 2 * ncol]
    parent_ref, lower_ref, dinv_ref, x_ref, z_ref, e_ref, rh_ref, rl_ref, fh_ref, fl_ref, sel_ref = refs[
        2 * ncol :
    ]
    base, own, c = slots(nrow, ncol)
    depth = f_refs[0].shape[0]
    rows = x_ref.shape[0]
    block = dinv_ref.shape[0]
    fold = depth // block
    chosen = parent_ref[c] ^ c
    for t in range(ncol):
        slot = base ^ t
        fh_ref[slot], fl_ref[slot] = split(f_refs[t][...])
    total = None
    for j in range(ncol):
        parts = split(r_refs[j][:rows])
        rh_ref[j], rl_ref[j] = parts
        term = dot_split(parts, (fh_ref[j], fl_ref[j]), NN)
        total = term if total is None else total + term
    x = -total
    x_ref[...] = x
    z_ref[:rows] = x
    diag = None
    for i, slot in enumerate(own):
        term = dot_split(
            (fh_ref[slot], fl_ref[slot]), split(total[i * depth : (i + 1) * depth]), TN
        )
        diag = term if diag is None else diag + term
    z_ref[rows:] = diag
    for j in range(ncol):

        @pl.when(chosen == j)
        def _(j=j):
            for i in range(fold):
                sel_ref[i * (block // fold) : (i + 1) * (block // fold)] = r_refs[j][
                    rows:, i * block : (i + 1) * block
                ]

    lower = split(lower_ref[...])
    product = dot_split(split(sel_ref[...]), lower, NN)
    e_ref[...] = dinv_ref[...] + dot_split(lower, split(product), TN)


def parent_kernel(z_ref, parent_ref, lower_ref, c_ref, t_ref):
    rows, block = c_ref.shape
    height = rows + block
    first = pl.multiple_of(parent_ref[lax.axis_index("col")] * height, block)
    lower = split(lower_ref[...])
    product = dot_split(split(z_ref[pl.ds(first, height)]), lower, NN)
    c_ref[...] = product[:rows]
    t_ref[...] = dot_split(lower, split(product[rows:]), TN)


def second_kernel(nrow, ncol, *refs):
    s_refs = refs[:ncol]
    rh_ref, rl_ref, c_ref, t_ref, z_ref, y_ref, m_ref, sh_ref, sl_ref = refs[ncol:]
    base, own, _ = slots(nrow, ncol)
    depth = s_refs[0].shape[0]
    for t in range(ncol):
        slot = base ^ t
        sh_ref[slot], sl_ref[slot] = split(s_refs[t][...])
    total = c_ref[...]
    for j in range(ncol):
        total += dot_split((rh_ref[j], rl_ref[j]), (sh_ref[j], sl_ref[j]), NN)
    y_ref[...] = -total
    coupling = c_ref[...]
    diag = t_ref[...]
    for i, slot in enumerate(own):
        mine = (sh_ref[slot], sl_ref[slot])
        here = slice(i * depth, (i + 1) * depth)
        diag += dot_split(mine, split(total[here]), TN)
        diag += dot_split(split(coupling[here]), mine, TN)
    rows = c_ref.shape[0]
    block = diag.shape[0]
    across = lax.broadcasted_iota(jnp.int32, diag.shape, 1)
    down = lax.broadcasted_iota(jnp.int32, diag.shape, 0)
    m_ref[:block] = jnp.where(down <= across, z_ref[rows : rows + block], diag)
    line = jnp.sum(jnp.where(down == across, diag, 0.0), axis=0, keepdims=True)
    m_ref[block:] = jnp.broadcast_to(line, (m_ref.shape[0] - block, line.shape[1]))


def last_kernel(m_ref, dinv_ref, e_ref, one_ref, two_ref):
    block = dinv_ref.shape[0]
    m = m_ref[:block]
    across = lax.broadcasted_iota(jnp.int32, m.shape, 1)
    down = lax.broadcasted_iota(jnp.int32, m.shape, 0)
    turned = m.T
    one_ref[...] = dinv_ref[...] + jnp.where(down <= across, m, turned)
    line = jnp.broadcast_to(m_ref[block : block + 1], m.shape)
    two_ref[...] = e_ref[...] + jnp.where(
        down == across, line, jnp.where(down > across, m, turned)
    )


def call(kernel, outs, scratch, *args, flops=0):
    size = 0
    for shape, dtype in [(a.shape, a.dtype) for a in args] + outs + scratch:
        if len(shape) > 1:
            count = 1
            for extent in shape:
                count *= extent
            size += count * jnp.dtype(dtype).itemsize
    limit = min(56 << 20, 3 * size + (4 << 20))
    return pl.pallas_call(
        kernel,
        out_shape=[jax.ShapeDtypeStruct(shape, dtype) for shape, dtype in outs],
        in_specs=[SMEM if a.ndim == 1 else VMEM for a in args],
        out_specs=[VMEM] * len(outs),
        scratch_shapes=[pltpu.VMEM(shape, dtype) for shape, dtype in scratch],
        compiler_params=pltpu.CompilerParams(vmem_limit_bytes=limit),
        cost_estimate=pl.CostEstimate(flops=flops, bytes_accessed=size, transcendentals=0),
    )(*args)


def masked(values, pattern):
    rows, cols = pattern.shape
    grid = values.reshape(rows, values.shape[0] // rows, cols, values.shape[1] // cols)
    return (grid * pattern.astype(jnp.float32)[:, None, :, None]).reshape(values.shape)


def swap(x, axis, size, bit):
    return lax.ppermute(x, axis, [(i, i ^ bit) for i in range(size)])


def gather_xor(x, axis, size):
    blocks = {0: x}
    bit = size // 2
    while bit:
        for j in sorted(blocks):
            blocks[j ^ bit] = swap(blocks[j], axis, size, bit)
        bit //= 2
    return [blocks[j] for j in range(size)]


def turn(values, nrow, ncol, block):
    q = ncol // nrow
    out = []
    for t in range(ncol):
        pairs = []
        for r in range(nrow):
            for c in range(ncol):
                k = (r * q + c % q) ^ t
                pairs.append(((c // q) * ncol + k, r * ncol + c))
        part = values
        if q > 1:
            which = (lax.axis_index("col") ^ t) % q
            part = lax.dynamic_slice_in_dim(values, which * block, block, 1)
        out.append(lax.ppermute(part, ("row", "col"), pairs))
    return out


def on_device(
    nrow,
    ncol,
    inverse_root,
    lower_first,
    mask_first,
    dinv_first,
    lower_second,
    mask_second,
    parent,
    lower_parent,
    dinv_second,
):
    f32, bf16 = jnp.float32, jnp.bfloat16
    block = dinv_first.shape[0]
    rows, depth = inverse_root.shape
    first = masked(lower_first, mask_first)
    second = masked(lower_second, mask_second)
    f_parts = turn(first, nrow, ncol, block)
    fold = depth // block
    folded = jnp.concatenate(
        [dinv_first[i * (block // fold) : (i + 1) * (block // fold)] for i in range(fold)], 1
    )
    r_parts = gather_xor(jnp.concatenate([inverse_root, folded], 0), "col", ncol)
    s_parts = turn(second, nrow, ncol, block)
    halves = [((ncol, rows, depth), bf16)] * 2
    pieces = [((ncol, depth, block), bf16)] * 2
    inverse_first, z, start, r_high, r_low = call(
        functools.partial(first_kernel, nrow, ncol),
        [((rows, block), f32), ((rows + block, block), f32), ((block, block), f32)] + halves,
        pieces + [((block, block), f32)],
        *r_parts,
        *f_parts,
        parent,
        lower_parent,
        dinv_second,
    )
    coupling, parent_diag = call(
        parent_kernel,
        [((rows, block), f32), ((block, block), f32)],
        [],
        lax.all_gather(z, "col", axis=0, tiled=True),
        parent,
        lower_parent,
    )
    inverse_second, packed = call(
        functools.partial(second_kernel, nrow, ncol),
        [((rows, block), f32), ((block + 8, block), f32)],
        pieces,
        *s_parts,
        r_high,
        r_low,
        coupling,
        parent_diag,
        z,
    )
    bit = 1
    while bit < nrow:
        packed = packed + swap(packed, "row", nrow, bit)
        bit *= 2
    diag_first, diag_second = call(
        last_kernel, [((block, block), f32)] * 2, [], packed, dinv_first, start
    )
    return (inverse_first, diag_first, inverse_second, diag_second)


def solution(mesh):
    in_specs = (
        P(("pole", "row"), "col"),
        P(("pole", "col"), "row"),
        P("col", "row"),
        P("pole", "col"),
        P(("pole", "col"), "row"),
        P("col", "row"),
        P(),
        P("pole", "col"),
        P("pole", "col"),
    )
    out_specs = (
        P(("pole", "row"), "col"),
        P("pole", "col"),
        P(("pole", "row"), "col"),
        P("pole", "col"),
    )
    return jax.shard_map(
        functools.partial(on_device, mesh.shape["row"], mesh.shape["col"]),
        mesh=mesh,
        in_specs=in_specs,
        out_specs=out_specs,
        check_vma=False,
    )
```

```python
import functools

import jax
import jax.numpy as jnp
from jax import lax
from jax.experimental import pallas as pl
from jax.experimental.pallas import tpu as pltpu
from jax.sharding import PartitionSpec as P

VMEM = pl.BlockSpec(memory_space=pltpu.VMEM)
SMEM = pl.BlockSpec(memory_space=pltpu.SMEM)
NN = ((1,), (0,))
TN = ((0,), (0,))
BLOCK = 128
PIECES = 2


def split(x):
    high = x.astype(jnp.bfloat16)
    return high, (x - high.astype(jnp.float32)).astype(jnp.bfloat16)


def dot_split(a, b, dims):
    def one(left, right):
        return lax.dot_general(left, right, (dims, ((), ())), preferred_element_type=jnp.float32)

    return one(a[0], b[0]) + (one(a[0], b[1]) + one(a[1], b[0]))


def dot3(a, b, dims=NN):
    return dot_split(split(a), split(b), dims)


def slots(nrow, ncol):
    q = ncol // nrow
    r, c = lax.axis_index("row"), lax.axis_index("col")
    own = [(r * q + i) ^ c for i in range(q)]
    return (r * q + c % q) ^ c, own, c


def prepare_kernel(
    root_ref, dinv_ref, first_ref, second_ref, one_ref, two_ref, panel_ref, both_ref, raw_ref, sems
):
    rows, depth = root_ref.shape
    block = dinv_ref.shape[0]
    fold = depth // block
    part = block // fold
    high, width = first_ref.shape
    across = width // BLOCK
    loads = [(first_ref, raw_ref.at[:high]), (second_ref, raw_ref.at[high:])]
    loads.append((root_ref, panel_ref.at[:rows]))
    for i in range(fold):
        cols = pl.ds(i * block, block)
        loads.append((dinv_ref.at[pl.ds(i * part, part)], panel_ref.at[pl.ds(rows, part), cols]))
    copies = [pltpu.make_async_copy(src, dst, sems.at[i]) for i, (src, dst) in enumerate(loads)]
    for copy in copies:
        copy.start()
    for level, pattern_ref in enumerate((one_ref, two_ref)):
        copies[level].wait()
        for i in range(high // BLOCK):
            here = slice(level * high + i * BLOCK, level * high + (i + 1) * BLOCK)
            for j in range(across):
                cols = slice(j * BLOCK, (j + 1) * BLOCK)
                factor = pattern_ref[i * across + j].astype(jnp.float32)
                both_ref[here, cols] = raw_ref[here, cols] * factor
    for copy in copies[2:]:
        copy.wait()


def pair_kernel(level, own_ref, other_ref, *refs):
    out_ref = refs[-1]
    depth = own_ref.shape[0] // 2
    here = slice(level * depth, (level + 1) * depth)
    out_ref[:depth] = own_ref[here]
    out_ref[depth:] = other_ref[here]


def first_kernel(nrow, ncol, *refs):
    pairs = ncol // 2
    count = pairs * (1 + PIECES)
    r_refs, f_refs = refs[:count], refs[count : count + pairs]
    parent_ref, lower_ref, dinv_ref, x_ref, z_ref, e_ref, rh_ref, rl_ref, fh_ref, fl_ref, sel_ref = refs[
        count + pairs :
    ]
    base, own, c = slots(nrow, ncol)
    depth = f_refs[0].shape[0] // 2
    rows = x_ref.shape[0]
    block = dinv_ref.shape[0]
    fold = depth // block
    chosen = parent_ref[c] ^ c
    for t in range(ncol):
        slot = base ^ t
        part = f_refs[t // 2][t % 2 * depth : (t % 2 + 1) * depth]
        fh_ref[slot], fl_ref[slot] = split(part)
    total = None
    for j in range(ncol):
        first = j // 2 * (1 + PIECES)
        start = 0
        for ref in r_refs[first + 1 : first + 1 + PIECES] if j % 2 else r_refs[first : first + 1]:
            stop = min(start + ref.shape[0], rows)
            if start < stop:
                rh_ref[j, start:stop], rl_ref[j, start:stop] = split(ref[: stop - start])
            start = stop
        term = dot_split((rh_ref[j], rl_ref[j]), (fh_ref[j], fl_ref[j]), NN)
        total = term if total is None else total + term
    x = -total
    x_ref[...] = x
    z_ref[:rows] = x
    diag = None
    for i, slot in enumerate(own):
        term = dot_split(
            (fh_ref[slot], fl_ref[slot]), split(total[i * depth : (i + 1) * depth]), TN
        )
        diag = term if diag is None else diag + term
    z_ref[rows:] = diag
    for j in range(ncol):

        @pl.when(chosen == j)
        def _(j=j):
            for i in range(fold):
                sel_ref[i * (block // fold) : (i + 1) * (block // fold)] = r_refs[
                    j // 2 * (1 + PIECES) + j % 2 * PIECES
                ][-(block // fold) :, i * block : (i + 1) * block]

    lower = split(lower_ref[...])
    product = dot_split(split(sel_ref[...]), lower, NN)
    e_ref[...] = dinv_ref[...] + dot_split(lower, split(product), TN)


def parent_kernel(z_ref, parent_ref, lower_ref, c_ref, t_ref):
    rows, block = c_ref.shape
    height = rows + block
    first = pl.multiple_of(parent_ref[lax.axis_index("col")] * height, block)
    lower = split(lower_ref[...])
    product = dot_split(split(z_ref[pl.ds(first, height)]), lower, NN)
    c_ref[...] = product[:rows]
    t_ref[...] = dot_split(lower, split(product[rows:]), TN)


def second_kernel(nrow, ncol, *refs):
    pairs = ncol // 2
    s_refs = refs[:pairs]
    rh_ref, rl_ref, c_ref, t_ref, z_ref, y_ref, m_ref, sh_ref, sl_ref = refs[pairs:]
    base, own, _ = slots(nrow, ncol)
    depth = s_refs[0].shape[0] // 2
    for t in range(ncol):
        slot = base ^ t
        part = s_refs[t // 2][t % 2 * depth : (t % 2 + 1) * depth]
        sh_ref[slot], sl_ref[slot] = split(part)
    total = c_ref[...]
    for j in range(ncol):
        total += dot_split((rh_ref[j], rl_ref[j]), (sh_ref[j], sl_ref[j]), NN)
    y_ref[...] = -total
    coupling = c_ref[...]
    diag = t_ref[...]
    for i, slot in enumerate(own):
        mine = (sh_ref[slot], sl_ref[slot])
        here = slice(i * depth, (i + 1) * depth)
        diag += dot_split(mine, split(total[here]), TN)
        diag += dot_split(split(coupling[here]), mine, TN)
    rows = c_ref.shape[0]
    block = diag.shape[0]
    across = lax.broadcasted_iota(jnp.int32, diag.shape, 1)
    down = lax.broadcasted_iota(jnp.int32, diag.shape, 0)
    m_ref[:block] = jnp.where(down <= across, z_ref[rows : rows + block], diag)
    line = jnp.sum(jnp.where(down == across, diag, 0.0), axis=0, keepdims=True)
    m_ref[block:] = jnp.broadcast_to(line, (m_ref.shape[0] - block, line.shape[1]))


def last_kernel(m_ref, dinv_ref, e_ref, one_ref, two_ref):
    block = dinv_ref.shape[0]
    m = m_ref[:block]
    across = lax.broadcasted_iota(jnp.int32, m.shape, 1)
    down = lax.broadcasted_iota(jnp.int32, m.shape, 0)
    turned = m.T
    one_ref[...] = dinv_ref[...] + jnp.where(down <= across, m, turned)
    line = jnp.broadcast_to(m_ref[block : block + 1], m.shape)
    two_ref[...] = e_ref[...] + jnp.where(
        down == across, line, jnp.where(down > across, m, turned)
    )


def call(kernel, outs, scratch, *args, flops=0):
    size = 0
    for shape, dtype in [(a.shape, a.dtype) for a in args] + outs + scratch:
        if len(shape) > 1:
            count = 1
            for extent in shape:
                count *= extent
            size += count * jnp.dtype(dtype).itemsize
    limit = min(56 << 20, 3 * size + (4 << 20))
    return pl.pallas_call(
        kernel,
        out_shape=[jax.ShapeDtypeStruct(shape, dtype) for shape, dtype in outs],
        in_specs=[SMEM if a.ndim == 1 else VMEM for a in args],
        out_specs=[VMEM] * len(outs),
        scratch_shapes=[pltpu.VMEM(shape, dtype) for shape, dtype in scratch],
        compiler_params=pltpu.CompilerParams(vmem_limit_bytes=limit),
        cost_estimate=pl.CostEstimate(flops=flops, bytes_accessed=size, transcendentals=0),
    )(*args)


def swap(x, axis, size, bit):
    return lax.ppermute(x, axis, [(i, i ^ bit) for i in range(size)])


def gather_xor(x, axis, size):
    blocks = {0: x}
    bit = size // 2
    while bit:
        for j in sorted(blocks):
            if bit > 1:
                blocks[j ^ bit] = swap(blocks[j], axis, size, bit)
        bit //= 2
    parts = []
    for j in range(0, size, 2):
        parts.append(blocks[j])
        count = blocks[j].shape[0] // PIECES
        parts += [
            swap(blocks[j][i * count : (i + 1) * count], axis, size, 1) for i in range(PIECES)
        ]
    return parts


def turn(values, nrow, ncol, block):
    q = ncol // nrow
    out = []
    for t in range(0, ncol, 2):
        pairs = []
        for r in range(nrow):
            for c in range(ncol):
                k = (r * q + c % q) ^ t
                pairs.append(((c // q) * ncol + k, r * ncol + c))
        part = values
        if q > 1:
            which = (lax.axis_index("col") ^ t) % q
            part = lax.dynamic_slice_in_dim(values, which * block, block, 1)
        out.append(lax.ppermute(part, ("row", "col"), pairs))
    return out


def on_device(
    nrow,
    ncol,
    inverse_root,
    lower_first,
    mask_first,
    dinv_first,
    lower_second,
    mask_second,
    parent,
    lower_parent,
    dinv_second,
):
    f32, bf16 = jnp.float32, jnp.bfloat16
    block = dinv_first.shape[0]
    rows, depth = inverse_root.shape
    fold = depth // block
    tall = (2 * lower_first.shape[0], lower_first.shape[1])
    anywhere = pl.BlockSpec(memory_space=pl.ANY)
    panel, both = pl.pallas_call(
        prepare_kernel,
        out_shape=[
            jax.ShapeDtypeStruct((rows + block // fold, depth), f32),
            jax.ShapeDtypeStruct(tall, f32),
        ],
        in_specs=[anywhere] * 4 + [SMEM] * 2,
        out_specs=[VMEM] * 2,
        scratch_shapes=[pltpu.VMEM(tall, f32), pltpu.SemaphoreType.DMA((3 + fold,))],
    )(
        inverse_root,
        dinv_first,
        lower_first,
        lower_second,
        mask_first.reshape(-1),
        mask_second.reshape(-1),
    )
    other = swap(both, "col", ncol, 1)
    first = call(functools.partial(pair_kernel, 0), [(both.shape, f32)], [], both, other)[0]
    f_parts = turn(first, nrow, ncol, block)
    r_parts = gather_xor(panel, "col", ncol)
    second = call(
        functools.partial(pair_kernel, 1), [(both.shape, f32)], [], both, other
    )[0]
    s_parts = turn(second, nrow, ncol, block)
    halves = [((ncol, rows, depth), bf16)] * 2
    pieces = [((ncol, depth, block), bf16)] * 2
    inverse_first, z, start, r_high, r_low = call(
        functools.partial(first_kernel, nrow, ncol),
        [((rows, block), f32), ((rows + block, block), f32), ((block, block), f32)] + halves,
        pieces + [((block, block), f32)],
        *r_parts,
        *f_parts,
        parent,
        lower_parent,
        dinv_second,
    )
    coupling, parent_diag = call(
        parent_kernel,
        [((rows, block), f32), ((block, block), f32)],
        [],
        lax.all_gather(z, "col", axis=0, tiled=True),
        parent,
        lower_parent,
    )
    inverse_second, packed = call(
        functools.partial(second_kernel, nrow, ncol),
        [((rows, block), f32), ((block + 8, block), f32)],
        pieces,
        *s_parts,
        r_high,
        r_low,
        coupling,
        parent_diag,
        z,
    )
    bit = 1
    while bit < nrow:
        packed = packed + swap(packed, "row", nrow, bit)
        bit *= 2
    diag_first, diag_second = call(
        last_kernel, [((block, block), f32)] * 2, [], packed, dinv_first, start
    )
    return (inverse_first, diag_first, inverse_second, diag_second)


def solution(mesh):
    in_specs = (
        P(("pole", "row"), "col"),
        P(("pole", "col"), "row"),
        P("col", "row"),
        P("pole", "col"),
        P(("pole", "col"), "row"),
        P("col", "row"),
        P(),
        P("pole", "col"),
        P("pole", "col"),
    )
    out_specs = (
        P(("pole", "row"), "col"),
        P("pole", "col"),
        P(("pole", "row"), "col"),
        P("pole", "col"),
    )
    return jax.shard_map(
        functools.partial(on_device, mesh.shape["row"], mesh.shape["col"]),
        mesh=mesh,
        in_specs=in_specs,
        out_specs=out_specs,
        check_vma=False,
    )
```

```python
import functools

import jax
import jax.numpy as jnp
from jax import lax
from jax.experimental import pallas as pl
from jax.experimental.pallas import tpu as pltpu
from jax.sharding import PartitionSpec as P

VMEM = pl.BlockSpec(memory_space=pltpu.VMEM)
SMEM = pl.BlockSpec(memory_space=pltpu.SMEM)
NN = ((1,), (0,))
TN = ((0,), (0,))
BLOCK = 128
PIECES = 2


def split(x):
    high = x.astype(jnp.bfloat16)
    return high, (x - high.astype(jnp.float32)).astype(jnp.bfloat16)


def dot_split(a, b, dims):
    def one(left, right):
        return lax.dot_general(left, right, (dims, ((), ())), preferred_element_type=jnp.float32)

    return one(a[0], b[0]) + (one(a[0], b[1]) + one(a[1], b[0]))


def dot3(a, b, dims=NN):
    return dot_split(split(a), split(b), dims)


def slots(nrow, ncol):
    q = ncol // nrow
    r, c = lax.axis_index("row"), lax.axis_index("col")
    own = [(r * q + i) ^ c for i in range(q)]
    return (r * q + c % q) ^ c, own, c


def prepare_kernel(
    root_ref, dinv_ref, first_ref, second_ref, one_ref, two_ref, panel_ref, both_ref, raw_ref, sems
):
    rows, depth = root_ref.shape
    block = dinv_ref.shape[0]
    fold = depth // block
    part = block // fold
    high, width = first_ref.shape
    across = width // BLOCK
    loads = [(first_ref, raw_ref.at[:high]), (second_ref, raw_ref.at[high:])]
    loads.append((root_ref, panel_ref.at[:rows]))
    for i in range(fold):
        cols = pl.ds(i * block, block)
        loads.append((dinv_ref.at[pl.ds(i * part, part)], panel_ref.at[pl.ds(rows, part), cols]))
    copies = [pltpu.make_async_copy(src, dst, sems.at[i]) for i, (src, dst) in enumerate(loads)]
    for copy in copies:
        copy.start()
    for level, pattern_ref in enumerate((one_ref, two_ref)):
        copies[level].wait()
        for i in range(high // BLOCK):
            here = slice(level * high + i * BLOCK, level * high + (i + 1) * BLOCK)
            for j in range(across):
                cols = slice(j * BLOCK, (j + 1) * BLOCK)
                factor = pattern_ref[i * across + j].astype(jnp.float32)
                both_ref[here, cols] = raw_ref[here, cols] * factor
    for copy in copies[2:]:
        copy.wait()


def pair_kernel(level, own_ref, other_ref, *refs):
    out_ref = refs[-1]
    depth = own_ref.shape[0] // 2
    here = slice(level * depth, (level + 1) * depth)
    out_ref[:depth] = own_ref[here]
    out_ref[depth:] = other_ref[here]


def panel_kernel(nrow, ncol, *refs):
    count = ncol // 2 * (1 + PIECES)
    r_refs = refs[:count]
    parent_ref, lower_ref, dinv_ref, e_ref, rh_ref, rl_ref, sel_ref = refs[count:]
    _, rows, depth = rh_ref.shape
    block = dinv_ref.shape[0]
    fold = depth // block
    part = block // fold
    c = lax.axis_index("col")
    chosen = parent_ref[c] ^ c
    for j in range(ncol):
        first = j // 2 * (1 + PIECES)
        here = r_refs[first + 1 : first + 1 + PIECES] if j % 2 else r_refs[first : first + 1]
        start = 0
        for ref in here:
            stop = min(start + ref.shape[0], rows)
            if start < stop:
                rh_ref[j, start:stop], rl_ref[j, start:stop] = split(ref[: stop - start])
            start = stop

        @pl.when(chosen == j)
        def _(last=here[-1]):
            for i in range(fold):
                sel_ref[i * part : (i + 1) * part] = last[-part:, i * block : (i + 1) * block]

    lower = split(lower_ref[...])
    product = dot_split(split(sel_ref[...]), lower, NN)
    e_ref[...] = dinv_ref[...] + dot_split(lower, split(product), TN)


def spread(nrow, ncol, refs, high_ref, low_ref):
    base, own, _ = slots(nrow, ncol)
    depth = refs[0].shape[0] // 2
    for t in range(ncol):
        slot = base ^ t
        part = refs[-1 - t // 2][t % 2 * depth : (t % 2 + 1) * depth]
        high_ref[slot], low_ref[slot] = split(part)
    return own, depth


def first_kernel(nrow, ncol, *refs):
    f_refs = refs[: ncol // 2]
    rh_ref, rl_ref, x_ref, z_ref, fh_ref, fl_ref = refs[ncol // 2 :]
    own, depth = spread(nrow, ncol, f_refs, fh_ref, fl_ref)
    total = None
    for j in range(ncol):
        term = dot_split((rh_ref[j], rl_ref[j]), (fh_ref[j], fl_ref[j]), NN)
        total = term if total is None else total + term
    x = -total
    x_ref[...] = x
    rows = x.shape[0]
    z_ref[:rows] = x
    diag = None
    for i, slot in enumerate(own):
        term = dot_split(
            (fh_ref[slot], fl_ref[slot]), split(total[i * depth : (i + 1) * depth]), TN
        )
        diag = term if diag is None else diag + term
    z_ref[rows:] = diag


def second_kernel(nrow, ncol, *refs):
    s_refs = refs[: ncol // 2]
    rh_ref, rl_ref, all_ref, parent_ref, lower_ref, z_ref, y_ref, m_ref, sh_ref, sl_ref = refs[
        ncol // 2 :
    ]
    own, depth = spread(nrow, ncol, s_refs, sh_ref, sl_ref)
    rows = y_ref.shape[0]
    block = lower_ref.shape[0]
    height = rows + block
    first = pl.multiple_of(parent_ref[lax.axis_index("col")] * height, block)
    lower = split(lower_ref[...])
    product = dot_split(split(all_ref[pl.ds(first, height)]), lower, NN)
    coupling = product[:rows]
    diag = dot_split(lower, split(product[rows:]), TN)
    total = coupling
    for j in range(ncol):
        total += dot_split((rh_ref[j], rl_ref[j]), (sh_ref[j], sl_ref[j]), NN)
    y_ref[...] = -total
    for i, slot in enumerate(own):
        mine = (sh_ref[slot], sl_ref[slot])
        here = slice(i * depth, (i + 1) * depth)
        diag += dot_split(mine, split(total[here]), TN)
        diag += dot_split(split(coupling[here]), mine, TN)
    across = lax.broadcasted_iota(jnp.int32, diag.shape, 1)
    down = lax.broadcasted_iota(jnp.int32, diag.shape, 0)
    m_ref[:block] = jnp.where(down <= across, z_ref[rows : rows + block], diag)
    line = jnp.sum(jnp.where(down == across, diag, 0.0), axis=0, keepdims=True)
    m_ref[block:] = jnp.broadcast_to(line, (m_ref.shape[0] - block, line.shape[1]))


def last_kernel(dinv_ref, e_ref, *refs):
    one_ref, two_ref = refs[-2:]
    block = dinv_ref.shape[0]
    total = refs[0][...]
    for ref in refs[1:-2]:
        total += ref[...]
    m = total[:block]
    across = lax.broadcasted_iota(jnp.int32, m.shape, 1)
    down = lax.broadcasted_iota(jnp.int32, m.shape, 0)
    turned = m.T
    one_ref[...] = dinv_ref[...] + jnp.where(down <= across, m, turned)
    line = jnp.broadcast_to(total[block : block + 1], m.shape)
    two_ref[...] = e_ref[...] + jnp.where(
        down == across, line, jnp.where(down > across, m, turned)
    )


def call(kernel, outs, scratch, *args, flops=0):
    size = 0
    for shape, dtype in [(a.shape, a.dtype) for a in args] + outs + scratch:
        if len(shape) > 1:
            count = 1
            for extent in shape:
                count *= extent
            size += count * jnp.dtype(dtype).itemsize
    limit = min(56 << 20, 3 * size + (4 << 20))
    return pl.pallas_call(
        kernel,
        out_shape=[jax.ShapeDtypeStruct(shape, dtype) for shape, dtype in outs],
        in_specs=[SMEM if a.ndim == 1 else VMEM for a in args],
        out_specs=[VMEM] * len(outs),
        scratch_shapes=[pltpu.VMEM(shape, dtype) for shape, dtype in scratch],
        compiler_params=pltpu.CompilerParams(vmem_limit_bytes=limit),
        cost_estimate=pl.CostEstimate(flops=flops, bytes_accessed=size, transcendentals=0),
    )(*args)


def swap(x, axis, size, bit):
    return lax.ppermute(x, axis, [(i, i ^ bit) for i in range(size)])


def gather_xor(x, axis, size):
    blocks = {0: x}
    bit = size // 2
    while bit:
        for j in sorted(blocks):
            if bit > 1:
                blocks[j ^ bit] = swap(blocks[j], axis, size, bit)
        bit //= 2
    parts = []
    for j in range(0, size, 2):
        parts.append(blocks[j])
        count = blocks[j].shape[0] // PIECES
        parts += [
            swap(blocks[j][i * count : (i + 1) * count], axis, size, 1) for i in range(PIECES)
        ]
    return parts


def turn(values, nrow, ncol, block):
    q = ncol // nrow
    out = []
    for t in range(0, ncol, 2):
        pairs = []
        for r in range(nrow):
            for c in range(ncol):
                k = (r * q + c % q) ^ t
                pairs.append(((c // q) * ncol + k, r * ncol + c))
        part = values
        if q > 1:
            which = (lax.axis_index("col") ^ t) % q
            part = lax.dynamic_slice_in_dim(values, which * block, block, 1)
        out.append(lax.ppermute(part, ("row", "col"), pairs))
    return out


def on_device(
    nrow,
    ncol,
    inverse_root,
    lower_first,
    mask_first,
    dinv_first,
    lower_second,
    mask_second,
    parent,
    lower_parent,
    dinv_second,
):
    f32, bf16 = jnp.float32, jnp.bfloat16
    block = dinv_first.shape[0]
    rows, depth = inverse_root.shape
    fold = depth // block
    tall = (2 * lower_first.shape[0], lower_first.shape[1])
    anywhere = pl.BlockSpec(memory_space=pl.ANY)
    panel, both = pl.pallas_call(
        prepare_kernel,
        out_shape=[
            jax.ShapeDtypeStruct((rows + block // fold, depth), f32),
            jax.ShapeDtypeStruct(tall, f32),
        ],
        in_specs=[anywhere] * 4 + [SMEM] * 2,
        out_specs=[VMEM] * 2,
        scratch_shapes=[pltpu.VMEM(tall, f32), pltpu.SemaphoreType.DMA((3 + fold,))],
    )(
        inverse_root,
        dinv_first,
        lower_first,
        lower_second,
        mask_first.reshape(-1),
        mask_second.reshape(-1),
    )
    other = swap(both, "col", ncol, 1)
    first = call(functools.partial(pair_kernel, 0), [(both.shape, f32)], [], both, other)[0]
    f_parts = turn(first, nrow, ncol, block)
    r_parts = gather_xor(panel, "col", ncol)
    second = call(
        functools.partial(pair_kernel, 1), [(both.shape, f32)], [], both, other
    )[0]
    s_parts = turn(second, nrow, ncol, block)
    halves = [((ncol, rows, depth), bf16)] * 2
    pieces = [((ncol, depth, block), bf16)] * 2
    start, r_high, r_low = call(
        functools.partial(panel_kernel, nrow, ncol),
        [((block, block), f32)] + halves,
        [((block, block), f32)],
        *r_parts,
        parent,
        lower_parent,
        dinv_second,
    )
    inverse_first, z = call(
        functools.partial(first_kernel, nrow, ncol),
        [((rows, block), f32), ((rows + block, block), f32)],
        pieces,
        *f_parts[::-1],
        r_high,
        r_low,
    )
    inverse_second, packed = call(
        functools.partial(second_kernel, nrow, ncol),
        [((rows, block), f32), ((block + 8, block), f32)],
        pieces,
        *s_parts[::-1],
        r_high,
        r_low,
        lax.all_gather(z, "col", axis=0, tiled=True),
        parent,
        lower_parent,
        z,
    )
    diag_first, diag_second = call(
        last_kernel,
        [((block, block), f32)] * 2,
        [],
        dinv_first,
        start,
        packed,
        *[swap(packed, "row", nrow, j) for j in range(nrow - 1, 0, -1)],
    )
    return (inverse_first, diag_first, inverse_second, diag_second)


def solution(mesh):
    in_specs = (
        P(("pole", "row"), "col"),
        P(("pole", "col"), "row"),
        P("col", "row"),
        P("pole", "col"),
        P(("pole", "col"), "row"),
        P("col", "row"),
        P(),
        P("pole", "col"),
        P("pole", "col"),
    )
    out_specs = (
        P(("pole", "row"), "col"),
        P("pole", "col"),
        P(("pole", "row"), "col"),
        P("pole", "col"),
    )
    return jax.shard_map(
        functools.partial(on_device, mesh.shape["row"], mesh.shape["col"]),
        mesh=mesh,
        in_specs=in_specs,
        out_specs=out_specs,
        check_vma=False,
    )
```

```python
import functools

import jax
import jax.numpy as jnp
from jax import lax
from jax.experimental import pallas as pl
from jax.experimental.pallas import tpu as pltpu
from jax.sharding import PartitionSpec as P

VMEM = pl.BlockSpec(memory_space=pltpu.VMEM)
SMEM = pl.BlockSpec(memory_space=pltpu.SMEM)
NN = ((1,), (0,))
TN = ((0,), (0,))
BLOCK = 128
PIECES = 2


def split(x):
    high = x.astype(jnp.bfloat16)
    return high, (x - high.astype(jnp.float32)).astype(jnp.bfloat16)


def dot_split(a, b, dims):
    def one(left, right):
        return lax.dot_general(left, right, (dims, ((), ())), preferred_element_type=jnp.float32)

    return one(a[0], b[0]) + (one(a[0], b[1]) + one(a[1], b[0]))


def dot3(a, b, dims=NN):
    return dot_split(split(a), split(b), dims)


def slots(nrow, ncol):
    q = ncol // nrow
    r, c = lax.axis_index("row"), lax.axis_index("col")
    own = [(r * q + i) ^ c for i in range(q)]
    return (r * q + c % q) ^ (c // q % 2 * (ncol // 2)) ^ c, own, c


def prepare_kernel(
    lower_ref, dinv_ref, first_ref, second_ref, one_ref, two_ref, side_ref, out1_ref, out2_ref, raw_ref, sems
):
    block = dinv_ref.shape[0]
    high, width = first_ref.shape
    across = width // BLOCK
    loads = [(first_ref, raw_ref.at[0]), (second_ref, raw_ref.at[1])]
    loads += [(lower_ref, side_ref.at[:block]), (dinv_ref, side_ref.at[block:])]
    copies = [pltpu.make_async_copy(src, dst, sems.at[i]) for i, (src, dst) in enumerate(loads)]
    for copy in copies:
        copy.start()
    for level, (pattern_ref, out_ref) in enumerate(((one_ref, out1_ref), (two_ref, out2_ref))):
        copies[level].wait()
        for i in range(high // BLOCK):
            rows = slice(i * BLOCK, (i + 1) * BLOCK)
            for j in range(across):
                cols = slice(j * BLOCK, (j + 1) * BLOCK)
                factor = pattern_ref[i * across + j].astype(jnp.float32)
                out_ref[rows, cols] = raw_ref[level, rows, cols] * factor
    for copy in copies[2:]:
        copy.wait()


def child_kernel(nrow, ncol, *refs):
    f_refs = refs[:nrow]
    second_ref, side_ref, parent_ref, sorted_ref, child_ref, held_ref = refs[nrow:]
    q = ncol // nrow
    depth = second_ref.shape[0]
    block = child_ref.shape[1] // q
    r, c = lax.axis_index("row"), lax.axis_index("col")
    for m in range(nrow):
        for j in range(q):
            held_ref[m * q + j] = f_refs[m][:, j * block : (j + 1) * block]
    for j in range(ncol):
        target = c ^ j
        sorted_ref[j * depth : (j + 1) * depth] = held_ref[((target // q) ^ r) * q + target % q]
    for j in range(q):
        mine = r * q + j
        above = parent_ref[mine]
        factor = held_ref[((above // q) ^ r) * q + above % q]
        lower = side_ref[pl.ds(pl.multiple_of(mine * 2 * block, block), block)]
        cols = slice(j * block, (j + 1) * block)
        child_ref[:, cols] = second_ref[:, cols] - dot3(factor, lower)


def pair_kernel(own_ref, other_ref, out_ref):
    depth = own_ref.shape[0]
    out_ref[:depth] = own_ref[...]
    out_ref[depth:] = other_ref[...]


def panel_kernel(nrow, ncol, *refs):
    count = ncol // 2 * (1 + PIECES)
    r_refs = refs[:count]
    side_ref, parent_ref, lower_ref, dinv_ref, e_ref, rh_ref, rl_ref = refs[count:]
    block = dinv_ref.shape[0]
    for j in range(ncol):
        first = j // 2 * (1 + PIECES)
        start = 0
        for ref in r_refs[first + 1 : first + 1 + PIECES] if j % 2 else r_refs[first : first + 1]:
            stop = start + ref.shape[0]
            rh_ref[j, start:stop], rl_ref[j, start:stop] = split(ref[...])
            start = stop
    above = parent_ref[lax.axis_index("col")]
    lower = split(lower_ref[...])
    dinv = side_ref[pl.ds(pl.multiple_of(above * 2 * block + block, block), block)]
    product = dot_split(split(dinv), lower, NN)
    e_ref[...] = dinv_ref[...] + dot_split(lower, split(product), TN)


def spread(nrow, ncol, refs, high_ref, low_ref):
    base, own, _ = slots(nrow, ncol)
    depth = refs[0].shape[0] // 2
    for t in range(ncol):
        slot = base ^ t
        part = refs[-1 - t // 2][t % 2 * depth : (t % 2 + 1) * depth]
        high_ref[slot], low_ref[slot] = split(part)
    return own, depth


def products(nrow, ncol, own, depth, r_refs, w_refs):
    total = None
    for j in range(ncol):
        term = dot_split((r_refs[0][j], r_refs[1][j]), (w_refs[0][j], w_refs[1][j]), NN)
        total = term if total is None else total + term
    diag = None
    for i, slot in enumerate(own):
        part = split(total[i * depth : (i + 1) * depth])
        term = dot_split((w_refs[0][slot], w_refs[1][slot]), part, TN)
        diag = term if diag is None else diag + term
    return total, diag


def first_kernel(nrow, ncol, *refs):
    rh_ref, rl_ref, x_ref, d_ref, fh_ref, fl_ref = refs[ncol:]
    own = slots(nrow, ncol)[1]
    depth = refs[0].shape[0]
    for j in range(ncol):
        fh_ref[j], fl_ref[j] = split(refs[j][...])
    total, diag = products(nrow, ncol, own, depth, (rh_ref, rl_ref), (fh_ref, fl_ref))
    x_ref[...] = -total
    d_ref[...] = diag


def second_kernel(nrow, ncol, *refs):
    rh_ref, rl_ref, d_ref, y_ref, m_ref, sh_ref, sl_ref = refs[ncol // 2 :]
    own, depth = spread(nrow, ncol, refs[: ncol // 2], sh_ref, sl_ref)
    total, diag = products(nrow, ncol, own, depth, (rh_ref, rl_ref), (sh_ref, sl_ref))
    y_ref[...] = -total
    block = diag.shape[0]
    across = lax.broadcasted_iota(jnp.int32, diag.shape, 1)
    down = lax.broadcasted_iota(jnp.int32, diag.shape, 0)
    m_ref[:block] = jnp.where(down <= across, d_ref[...], diag)
    line = jnp.sum(jnp.where(down == across, diag, 0.0), axis=0, keepdims=True)
    m_ref[block:] = jnp.broadcast_to(line, (m_ref.shape[0] - block, line.shape[1]))


def last_kernel(dinv_ref, e_ref, *refs):
    one_ref, two_ref = refs[-2:]
    block = dinv_ref.shape[0]
    total = refs[0][...]
    for ref in refs[1:-2]:
        total += ref[...]
    m = total[:block]
    across = lax.broadcasted_iota(jnp.int32, m.shape, 1)
    down = lax.broadcasted_iota(jnp.int32, m.shape, 0)
    turned = m.T
    one_ref[...] = dinv_ref[...] + jnp.where(down <= across, m, turned)
    line = jnp.broadcast_to(total[block : block + 1], m.shape)
    two_ref[...] = e_ref[...] + jnp.where(
        down == across, line, jnp.where(down > across, m, turned)
    )


def call(kernel, outs, scratch, *args, flops=0):
    size = 0
    for shape, dtype in [(a.shape, a.dtype) for a in args] + outs + scratch:
        if len(shape) > 1:
            count = 1
            for extent in shape:
                count *= extent
            size += count * jnp.dtype(dtype).itemsize
    limit = min(56 << 20, 3 * size + (4 << 20))
    return pl.pallas_call(
        kernel,
        out_shape=[jax.ShapeDtypeStruct(shape, dtype) for shape, dtype in outs],
        in_specs=[SMEM if a.ndim == 1 else VMEM for a in args],
        out_specs=[VMEM] * len(outs),
        scratch_shapes=[pltpu.VMEM(shape, dtype) for shape, dtype in scratch],
        compiler_params=pltpu.CompilerParams(vmem_limit_bytes=limit),
        cost_estimate=pl.CostEstimate(flops=flops, bytes_accessed=size, transcendentals=0),
    )(*args)


def swap(x, axis, size, bit):
    return lax.ppermute(x, axis, [(i, i ^ bit) for i in range(size)])


def gather_xor(x, axis, size):
    blocks = {0: x}
    bit = size // 2
    while bit:
        for j in sorted(blocks):
            if bit > 1:
                blocks[j ^ bit] = swap(blocks[j], axis, size, bit)
        bit //= 2
    parts = []
    for j in range(0, size, 2):
        parts.append(blocks[j])
        count = blocks[j].shape[0] // PIECES
        parts += [
            swap(blocks[j][i * count : (i + 1) * count], axis, size, 1) for i in range(PIECES)
        ]
    return parts


def after_kernel(value_ref, after_ref, out_ref):
    out_ref[...] = value_ref[...]


def after(value, other):
    return call(after_kernel, [(value.shape, jnp.float32)], [], value, other)[0]


def turn(values, nrow, ncol, block):
    q = ncol // nrow
    out = []
    for t in range(0, ncol, 2):
        pairs = []
        for r in range(nrow):
            for c in range(ncol):
                k = (r * q + c % q) ^ (c // q % 2 * (ncol // 2)) ^ t
                pairs.append(((c // q) * ncol + k, r * ncol + c))
        part = values
        if q > 1:
            which = (lax.axis_index("col") ^ t) % q
            part = lax.dynamic_slice_in_dim(values, which * block, block, 1)
        out.append(lax.ppermute(part, ("row", "col"), pairs))
    return out


def on_device(
    nrow,
    ncol,
    inverse_root,
    lower_first,
    mask_first,
    dinv_first,
    lower_second,
    mask_second,
    parent,
    lower_parent,
    dinv_second,
):
    f32, bf16 = jnp.float32, jnp.bfloat16
    block = dinv_first.shape[0]
    rows, depth = inverse_root.shape
    wide = lower_first.shape
    anywhere = pl.BlockSpec(memory_space=pl.ANY)
    side, first, second = pl.pallas_call(
        prepare_kernel,
        out_shape=[
            jax.ShapeDtypeStruct((2 * block, block), f32),
            jax.ShapeDtypeStruct(wide, f32),
            jax.ShapeDtypeStruct(wide, f32),
        ],
        in_specs=[anywhere] * 4 + [SMEM] * 2,
        out_specs=[VMEM] * 3,
        scratch_shapes=[pltpu.VMEM((2, *wide), f32), pltpu.SemaphoreType.DMA((4,))],
    )(
        lower_parent,
        dinv_first,
        lower_first,
        lower_second,
        mask_first.reshape(-1),
        mask_second.reshape(-1),
    )
    f_row = [first] + [swap(first, "row", nrow, m) for m in range(1, nrow)]
    sides = lax.all_gather(side, "col", axis=0, tiled=True)
    r_parts = gather_xor(after(inverse_root, sides), "col", ncol)
    ordered, child = call(
        functools.partial(child_kernel, nrow, ncol),
        [((ncol * depth, block), f32), (wide, f32)],
        [((ncol, depth, block), f32)],
        *f_row,
        second,
        sides,
        parent,
    )
    pair = call(
        pair_kernel, [((2 * depth, wide[1]), f32)], [], child, swap(child, "col", ncol, 1)
    )[0]
    g_parts = turn(pair, nrow, ncol, block)
    f_parts = {0: ordered}
    bit = ncol // 2
    while bit:
        for j in sorted(f_parts):
            here = f_parts[j]
            f_parts[j] = here[: bit * depth]
            sent = here[bit * depth :]
            f_parts[j ^ bit] = swap(after(sent, pair) if 2 * bit == ncol else sent, "col", ncol, bit)
        bit //= 2
    halves = [((ncol, rows, depth), bf16)] * 2
    pieces = [((ncol, depth, block), bf16)] * 2
    start, r_high, r_low = call(
        functools.partial(panel_kernel, nrow, ncol),
        [((block, block), f32)] + halves,
        [],
        *r_parts,
        sides,
        parent,
        lower_parent,
        dinv_second,
    )
    inverse_first, terms = call(
        functools.partial(first_kernel, nrow, ncol),
        [((rows, block), f32), ((block, block), f32)],
        pieces,
        *[f_parts[j] for j in range(ncol)],
        r_high,
        r_low,
    )
    inverse_second, packed = call(
        functools.partial(second_kernel, nrow, ncol),
        [((rows, block), f32), ((block + 8, block), f32)],
        pieces,
        *g_parts[::-1],
        r_high,
        r_low,
        terms,
    )
    diag_first, diag_second = call(
        last_kernel,
        [((block, block), f32)] * 2,
        [],
        dinv_first,
        start,
        packed,
        *[swap(packed, "row", nrow, j) for j in range(1, nrow)],
    )
    return (inverse_first, diag_first, inverse_second, diag_second)


def solution(mesh):
    in_specs = (
        P(("pole", "row"), "col"),
        P(("pole", "col"), "row"),
        P("col", "row"),
        P("pole", "col"),
        P(("pole", "col"), "row"),
        P("col", "row"),
        P(),
        P("pole", "col"),
        P("pole", "col"),
    )
    out_specs = (
        P(("pole", "row"), "col"),
        P("pole", "col"),
        P(("pole", "row"), "col"),
        P("pole", "col"),
    )
    return jax.shard_map(
        functools.partial(on_device, mesh.shape["row"], mesh.shape["col"]),
        mesh=mesh,
        in_specs=in_specs,
        out_specs=out_specs,
        check_vma=False,
    )
```

```python
import functools

import jax
import jax.numpy as jnp
from jax import lax
from jax.experimental import pallas as pl
from jax.experimental.pallas import tpu as pltpu
from jax.sharding import PartitionSpec as P

VMEM = pl.BlockSpec(memory_space=pltpu.VMEM)
SMEM = pl.BlockSpec(memory_space=pltpu.SMEM)
NN = ((1,), (0,))
TN = ((0,), (0,))
BLOCK = 128
PIECES = 2


def split(x):
    high = x.astype(jnp.bfloat16)
    return high, (x - high.astype(jnp.float32)).astype(jnp.bfloat16)


def dot_split(a, b, dims):
    def one(left, right):
        return lax.dot_general(left, right, (dims, ((), ())), preferred_element_type=jnp.float32)

    return one(a[0], b[0]) + (one(a[0], b[1]) + one(a[1], b[0]))


def dot3(a, b, dims=NN):
    return dot_split(split(a), split(b), dims)


def slots(nrow, ncol):
    q = ncol // nrow
    r, c = lax.axis_index("row"), lax.axis_index("col")
    own = [(r * q + i) ^ c for i in range(q)]
    return (r * q + c % q) ^ (c // q % 2 * (ncol // 2)) ^ c, own, c


def apply_mask(values_ref, pattern_ref, out_ref):
    high, width = values_ref.shape
    across = width // BLOCK
    for i in range(high // BLOCK):
        rows = slice(i * BLOCK, (i + 1) * BLOCK)
        for j in range(across):
            cols = slice(j * BLOCK, (j + 1) * BLOCK)
            factor = pattern_ref[i * across + j].astype(jnp.float32)
            out_ref[rows, cols] = values_ref[rows, cols] * factor


def mask_kernel(values_ref, pattern_ref, out_ref, raw_ref, sem):
    copy = pltpu.make_async_copy(values_ref, raw_ref, sem)
    copy.start()
    copy.wait()
    apply_mask(raw_ref, pattern_ref, out_ref)


def child_kernel(nrow, ncol, *refs):
    f_refs = refs[:nrow]
    second_ref, pattern_ref, side_ref, parent_ref, sorted_ref, child_ref, held_ref = refs[nrow:]
    q = ncol // nrow
    depth = second_ref.shape[0]
    block = child_ref.shape[1] // q
    r, c = lax.axis_index("row"), lax.axis_index("col")
    for m in range(nrow):
        for j in range(q):
            held_ref[(nrow - m) % nrow * q + j] = f_refs[m][:, j * block : (j + 1) * block]
    for j in range(ncol):
        target = c ^ j
        sorted_ref[j * depth : (j + 1) * depth] = held_ref[((target // q) ^ r) * q + target % q]
    apply_mask(second_ref, pattern_ref, child_ref)
    for j in range(q):
        mine = r * q + j
        above = parent_ref[mine]
        factor = held_ref[((above // q) ^ r) * q + above % q]
        lower = side_ref[pl.ds(pl.multiple_of(mine * block, block), block)]
        cols = slice(j * block, (j + 1) * block)
        child_ref[:, cols] -= dot3(factor, lower)


def pair_kernel(own_ref, other_ref, out_ref):
    depth = own_ref.shape[0]
    out_ref[:depth] = own_ref[...]
    out_ref[depth:] = other_ref[...]


def panel_kernel(nrow, ncol, *refs):
    count = ncol // 2 * (1 + PIECES)
    r_refs = refs[:count]
    parent_ref, lower_ref, dinv_ref, e_ref, rh_ref, rl_ref, sel_ref = refs[count:]
    _, rows, depth = rh_ref.shape
    block = dinv_ref.shape[0]
    part = block * block // depth
    c = lax.axis_index("col")
    chosen = parent_ref[c] ^ c
    for j in range(ncol):
        first = j // 2 * (1 + PIECES)
        here = r_refs[first + 1 : first + 1 + PIECES] if j % 2 else r_refs[first : first + 1]
        start = 0
        for ref in here:
            stop = min(start + ref.shape[0], rows)
            if start < stop:
                rh_ref[j, start:stop], rl_ref[j, start:stop] = split(ref[: stop - start])
            start = stop

        @pl.when(chosen == j)
        def _(last=here[-1]):
            for i in range(depth // block):
                sel_ref[i * part : (i + 1) * part] = last[-part:, i * block : (i + 1) * block]

    lower = split(lower_ref[...])
    product = dot_split(split(sel_ref[...]), lower, NN)
    e_ref[...] = dinv_ref[...] + dot_split(lower, split(product), TN)


def spread(nrow, ncol, refs, high_ref, low_ref):
    base, own, _ = slots(nrow, ncol)
    depth = refs[0].shape[0] // 2
    for t in range(ncol):
        slot = base ^ t
        part = refs[-1 - t // 2][t % 2 * depth : (t % 2 + 1) * depth]
        high_ref[slot], low_ref[slot] = split(part)
    return own, depth


def products(nrow, ncol, own, depth, r_refs, w_refs):
    total = None
    for j in range(ncol):
        term = dot_split((r_refs[0][j], r_refs[1][j]), (w_refs[0][j], w_refs[1][j]), NN)
        total = term if total is None else total + term
    diag = None
    for i, slot in enumerate(own):
        part = split(total[i * depth : (i + 1) * depth])
        term = dot_split((w_refs[0][slot], w_refs[1][slot]), part, TN)
        diag = term if diag is None else diag + term
    return total, diag


def first_kernel(nrow, ncol, *refs):
    rh_ref, rl_ref, x_ref, d_ref, fh_ref, fl_ref = refs[ncol:]
    own = slots(nrow, ncol)[1]
    depth = refs[0].shape[0]
    for j in range(ncol):
        fh_ref[j], fl_ref[j] = split(refs[j][...])
    total, diag = products(nrow, ncol, own, depth, (rh_ref, rl_ref), (fh_ref, fl_ref))
    x_ref[...] = -total
    d_ref[...] = diag


def second_kernel(nrow, ncol, *refs):
    rh_ref, rl_ref, d_ref, y_ref, m_ref, sh_ref, sl_ref = refs[ncol // 2 :]
    own, depth = spread(nrow, ncol, refs[: ncol // 2], sh_ref, sl_ref)
    total, diag = products(nrow, ncol, own, depth, (rh_ref, rl_ref), (sh_ref, sl_ref))
    y_ref[...] = -total
    block = diag.shape[0]
    across = lax.broadcasted_iota(jnp.int32, diag.shape, 1)
    down = lax.broadcasted_iota(jnp.int32, diag.shape, 0)
    m_ref[:block] = jnp.where(down <= across, d_ref[...], diag)
    line = jnp.sum(jnp.where(down == across, diag, 0.0), axis=0, keepdims=True)
    m_ref[block:] = jnp.broadcast_to(line, (m_ref.shape[0] - block, line.shape[1]))


def last_kernel(dinv_ref, e_ref, *refs):
    one_ref, two_ref = refs[-2:]
    block = dinv_ref.shape[0]
    total = refs[0][...]
    for ref in refs[1:-2]:
        total += ref[...]
    m = total[:block]
    across = lax.broadcasted_iota(jnp.int32, m.shape, 1)
    down = lax.broadcasted_iota(jnp.int32, m.shape, 0)
    turned = m.T
    one_ref[...] = dinv_ref[...] + jnp.where(down <= across, m, turned)
    line = jnp.broadcast_to(total[block : block + 1], m.shape)
    two_ref[...] = e_ref[...] + jnp.where(
        down == across, line, jnp.where(down > across, m, turned)
    )


def call(kernel, outs, scratch, *args, flops=0):
    size = 0
    for shape, dtype in [(a.shape, a.dtype) for a in args] + outs + scratch:
        if len(shape) > 1:
            count = 1
            for extent in shape:
                count *= extent
            size += count * jnp.dtype(dtype).itemsize
    limit = min(56 << 20, 3 * size + (4 << 20))
    return pl.pallas_call(
        kernel,
        out_shape=[jax.ShapeDtypeStruct(shape, dtype) for shape, dtype in outs],
        in_specs=[SMEM if a.ndim == 1 else VMEM for a in args],
        out_specs=[VMEM] * len(outs),
        scratch_shapes=[pltpu.VMEM(shape, dtype) for shape, dtype in scratch],
        compiler_params=pltpu.CompilerParams(vmem_limit_bytes=limit),
        cost_estimate=pl.CostEstimate(flops=flops, bytes_accessed=size, transcendentals=0),
    )(*args)


def swap(x, axis, size, bit):
    return lax.ppermute(x, axis, [(i, i ^ bit) for i in range(size)])


def gather_xor(x, axis, size):
    blocks = {0: x}
    bit = size // 2
    while bit:
        for j in sorted(blocks):
            if bit > 1:
                blocks[j ^ bit] = swap(blocks[j], axis, size, bit)
        bit //= 2
    parts = []
    for j in range(0, size, 2):
        parts.append(blocks[j])
        count = blocks[j].shape[0] // PIECES
        parts += [
            swap(blocks[j][i * count : (i + 1) * count], axis, size, 1) for i in range(PIECES)
        ]
    return parts


def fold_kernel(root_ref, dinv_ref, after_ref, out_ref):
    rows, depth = root_ref.shape
    block = dinv_ref.shape[0]
    part = block * block // depth
    out_ref[:rows] = root_ref[...]
    for i in range(depth // block):
        out_ref[rows:, i * block : (i + 1) * block] = dinv_ref[i * part : (i + 1) * part]


def after_kernel(value_ref, after_ref, out_ref):
    out_ref[...] = value_ref[...]


def after(value, other):
    return call(after_kernel, [(value.shape, jnp.float32)], [], value, other)[0]


def turn(values, nrow, ncol, block):
    q = ncol // nrow
    out = []
    for t in range(0, ncol, 2):
        pairs = []
        for r in range(nrow):
            for c in range(ncol):
                k = (r * q + c % q) ^ (c // q % 2 * (ncol // 2)) ^ t
                pairs.append(((c // q) * ncol + k, r * ncol + c))
        part = values
        if q > 1:
            which = (lax.axis_index("col") ^ t) % q
            part = lax.dynamic_slice_in_dim(values, which * block, block, 1)
        out.append(lax.ppermute(part, ("row", "col"), pairs))
    return out


def on_device(
    nrow,
    ncol,
    inverse_root,
    lower_first,
    mask_first,
    dinv_first,
    lower_second,
    mask_second,
    parent,
    lower_parent,
    dinv_second,
):
    f32, bf16 = jnp.float32, jnp.bfloat16
    block = dinv_first.shape[0]
    rows, depth = inverse_root.shape
    wide = lower_first.shape
    first = pl.pallas_call(
        mask_kernel,
        out_shape=jax.ShapeDtypeStruct(wide, f32),
        in_specs=[pl.BlockSpec(memory_space=pl.ANY), SMEM],
        out_specs=VMEM,
        scratch_shapes=[pltpu.VMEM(wide, f32), pltpu.SemaphoreType.DMA],
    )(lower_first, mask_first.reshape(-1))
    f_row = [first] + [swap(first, "row", nrow, m) for m in range(nrow - 1, 0, -1)]
    sides = lax.all_gather(lower_parent, "col", axis=0, tiled=True)
    tall = (rows + block * block // depth, depth)
    folded = call(fold_kernel, [(tall, f32)], [], inverse_root, dinv_first, sides)[0]
    r_parts = gather_xor(folded, "col", ncol)
    ordered, child = call(
        functools.partial(child_kernel, nrow, ncol),
        [((ncol * depth, block), f32), (wide, f32)],
        [((ncol, depth, block), f32)],
        *f_row,
        lower_second,
        mask_second.reshape(-1),
        sides,
        parent,
    )
    pair = call(
        pair_kernel, [((2 * depth, wide[1]), f32)], [], child, swap(child, "col", ncol, 1)
    )[0]
    g_parts = turn(pair, nrow, ncol, block)
    f_parts = {0: ordered}
    bit = ncol // 2
    while bit:
        for j in sorted(f_parts):
            here = f_parts[j]
            f_parts[j] = here[: bit * depth]
            sent = here[bit * depth :]
            f_parts[j ^ bit] = swap(after(sent, pair) if 2 * bit == ncol else sent, "col", ncol, bit)
        bit //= 2
    halves = [((ncol, rows, depth), bf16)] * 2
    pieces = [((ncol, depth, block), bf16)] * 2
    start, r_high, r_low = call(
        functools.partial(panel_kernel, nrow, ncol),
        [((block, block), f32)] + halves,
        [((block, block), f32)],
        *r_parts,
        parent,
        lower_parent,
        dinv_second,
    )
    inverse_first, terms = call(
        functools.partial(first_kernel, nrow, ncol),
        [((rows, block), f32), ((block, block), f32)],
        pieces,
        *[f_parts[j] for j in range(ncol)],
        r_high,
        r_low,
    )
    inverse_second, packed = call(
        functools.partial(second_kernel, nrow, ncol),
        [((rows, block), f32), ((block + 8, block), f32)],
        pieces,
        *g_parts[::-1],
        r_high,
        r_low,
        terms,
    )
    diag_first, diag_second = call(
        last_kernel,
        [((block, block), f32)] * 2,
        [],
        dinv_first,
        start,
        packed,
        *[swap(packed, "row", nrow, j) for j in range(1, nrow)],
    )
    return (inverse_first, diag_first, inverse_second, diag_second)


def solution(mesh):
    in_specs = (
        P(("pole", "row"), "col"),
        P(("pole", "col"), "row"),
        P("col", "row"),
        P("pole", "col"),
        P(("pole", "col"), "row"),
        P("col", "row"),
        P(),
        P("pole", "col"),
        P("pole", "col"),
    )
    out_specs = (
        P(("pole", "row"), "col"),
        P("pole", "col"),
        P(("pole", "row"), "col"),
        P("pole", "col"),
    )
    return jax.shard_map(
        functools.partial(on_device, mesh.shape["row"], mesh.shape["col"]),
        mesh=mesh,
        in_specs=in_specs,
        out_specs=out_specs,
        check_vma=False,
    )
```

```python
import functools

import jax
import jax.numpy as jnp
from jax import lax
from jax.experimental import pallas as pl
from jax.experimental.pallas import tpu as pltpu
from jax.sharding import PartitionSpec as P

VMEM = pl.BlockSpec(memory_space=pltpu.VMEM)
SMEM = pl.BlockSpec(memory_space=pltpu.SMEM)
NN = ((1,), (0,))
TN = ((0,), (0,))
BLOCK = 128
PIECES = 2


def split(x):
    high = x.astype(jnp.bfloat16)
    return high, (x - high.astype(jnp.float32)).astype(jnp.bfloat16)


def dot_split(a, b, dims):
    def one(left, right):
        return lax.dot_general(left, right, (dims, ((), ())), preferred_element_type=jnp.float32)

    return one(a[0], b[0]) + (one(a[0], b[1]) + one(a[1], b[0]))


def dot3(a, b, dims=NN):
    return dot_split(split(a), split(b), dims)


def slots(nrow, ncol):
    q = ncol // nrow
    r, c = lax.axis_index("row"), lax.axis_index("col")
    own = [(r * q + i) ^ c for i in range(q)]
    return (r * q + c % q) ^ (c // q % 2 * (ncol // 2)) ^ c, own, c


def apply_mask(values_ref, pattern_ref, out_ref):
    high, width = values_ref.shape
    across = width // BLOCK
    for i in range(high // BLOCK):
        rows = slice(i * BLOCK, (i + 1) * BLOCK)
        for j in range(across):
            cols = slice(j * BLOCK, (j + 1) * BLOCK)
            factor = pattern_ref[i * across + j].astype(jnp.float32)
            out_ref[rows, cols] = values_ref[rows, cols] * factor


def child_kernel(nrow, ncol, *refs):
    f_refs = refs[:nrow]
    second_ref, pattern_ref, side_ref, parent_ref, sorted_ref, child_ref, held_ref = refs[nrow:]
    q = ncol // nrow
    depth = second_ref.shape[0]
    block = child_ref.shape[1] // q
    r, c = lax.axis_index("row"), lax.axis_index("col")
    for m in range(nrow):
        for j in range(q):
            held_ref[(nrow - m) % nrow * q + j] = f_refs[m][:, j * block : (j + 1) * block]
    for j in range(ncol):
        target = c ^ j
        sorted_ref[j * depth : (j + 1) * depth] = held_ref[((target // q) ^ r) * q + target % q]
    apply_mask(second_ref, pattern_ref, child_ref)
    for j in range(q):
        mine = r * q + j
        above = parent_ref[mine]
        factor = held_ref[((above // q) ^ r) * q + above % q]
        lower = side_ref[pl.ds(pl.multiple_of(mine * block, block), block)]
        cols = slice(j * block, (j + 1) * block)
        child_ref[:, cols] -= dot3(factor, lower)


def pair_kernel(own_ref, other_ref, out_ref):
    depth = own_ref.shape[0]
    out_ref[:depth] = own_ref[...]
    out_ref[depth:] = other_ref[...]


def panel_kernel(nrow, ncol, *refs):
    count = ncol // 2 * (1 + PIECES)
    r_refs = refs[:count]
    parent_ref, lower_ref, dinv_ref, e_ref, rh_ref, rl_ref, sel_ref = refs[count:]
    _, rows, depth = rh_ref.shape
    block = dinv_ref.shape[0]
    part = block * block // depth
    c = lax.axis_index("col")
    chosen = parent_ref[c] ^ c
    for j in range(ncol):
        first = j // 2 * (1 + PIECES)
        here = r_refs[first + 1 : first + 1 + PIECES] if j % 2 else r_refs[first : first + 1]
        start = 0
        for ref in here:
            stop = min(start + ref.shape[0], rows)
            if start < stop:
                rh_ref[j, start:stop], rl_ref[j, start:stop] = split(ref[: stop - start])
            start = stop

        @pl.when(chosen == j)
        def _(last=here[-1]):
            for i in range(depth // block):
                sel_ref[i * part : (i + 1) * part] = last[-part:, i * block : (i + 1) * block]

    lower = split(lower_ref[...])
    product = dot_split(split(sel_ref[...]), lower, NN)
    e_ref[...] = dinv_ref[...] + dot_split(lower, split(product), TN)


def spread(nrow, ncol, refs, w_ref):
    base, own, _ = slots(nrow, ncol)
    depth = refs[0].shape[0] // 2
    block = w_ref.shape[2] // 2
    for t in range(ncol):
        slot = base ^ t
        part = refs[-1 - t // 2][t % 2 * depth : (t % 2 + 1) * depth]
        w_ref[slot, :, :block], w_ref[slot, :, block:] = split(part)
    return own, depth


def products(nrow, ncol, own, depth, r_refs, w_ref):
    block = w_ref.shape[2] // 2

    def one(left, right, dims):
        return lax.dot_general(left, right, (dims, ((), ())), preferred_element_type=jnp.float32)

    wide, rest = None, None
    for j in range(ncol):
        term = one(r_refs[0][j], w_ref[j], NN)
        wide = term if wide is None else wide + term
        term = one(r_refs[1][j], w_ref[j, :, :block], NN)
        rest = term if rest is None else rest + term
    total = wide[:, :block] + (wide[:, block:] + rest)
    diag = None
    for i, slot in enumerate(own):
        high, low = split(total[i * depth : (i + 1) * depth])
        tall = one(w_ref[slot], high, TN)
        term = tall[:block] + (tall[block:] + one(w_ref[slot, :, :block], low, TN))
        diag = term if diag is None else diag + term
    return total, diag


def first_kernel(nrow, ncol, *refs):
    rh_ref, rl_ref, x_ref, d_ref, w_ref = refs[ncol:]
    block = x_ref.shape[1]
    own = slots(nrow, ncol)[1]
    depth = refs[0].shape[0]
    for j in range(ncol):
        w_ref[j, :, :block], w_ref[j, :, block:] = split(refs[j][...])
    total, diag = products(nrow, ncol, own, depth, (rh_ref, rl_ref), w_ref)
    x_ref[...] = -total
    d_ref[...] = diag


def second_kernel(nrow, ncol, *refs):
    rh_ref, rl_ref, d_ref, y_ref, m_ref, w_ref = refs[ncol // 2 :]
    own, depth = spread(nrow, ncol, refs[: ncol // 2], w_ref)
    total, diag = products(nrow, ncol, own, depth, (rh_ref, rl_ref), w_ref)
    y_ref[...] = -total
    block = diag.shape[0]
    across = lax.broadcasted_iota(jnp.int32, diag.shape, 1)
    down = lax.broadcasted_iota(jnp.int32, diag.shape, 0)
    m_ref[:block] = jnp.where(down <= across, d_ref[...], diag)
    line = jnp.sum(jnp.where(down == across, diag, 0.0), axis=0, keepdims=True)
    m_ref[block:] = jnp.broadcast_to(line, (m_ref.shape[0] - block, line.shape[1]))


def last_kernel(dinv_ref, e_ref, *refs):
    one_ref, two_ref = refs[-2:]
    block = dinv_ref.shape[0]
    total = refs[0][...]
    for ref in refs[1:-2]:
        total += ref[...]
    m = total[:block]
    across = lax.broadcasted_iota(jnp.int32, m.shape, 1)
    down = lax.broadcasted_iota(jnp.int32, m.shape, 0)
    turned = m.T
    one_ref[...] = dinv_ref[...] + jnp.where(down <= across, m, turned)
    line = jnp.broadcast_to(total[block : block + 1], m.shape)
    two_ref[...] = e_ref[...] + jnp.where(
        down == across, line, jnp.where(down > across, m, turned)
    )


def call(kernel, outs, scratch, *args, flops=0):
    size = 0
    for shape, dtype in [(a.shape, a.dtype) for a in args] + outs + scratch:
        if len(shape) > 1:
            count = 1
            for extent in shape:
                count *= extent
            size += count * jnp.dtype(dtype).itemsize
    limit = min(56 << 20, 3 * size + (4 << 20))
    return pl.pallas_call(
        kernel,
        out_shape=[jax.ShapeDtypeStruct(shape, dtype) for shape, dtype in outs],
        in_specs=[SMEM if a.ndim == 1 else VMEM for a in args],
        out_specs=[VMEM] * len(outs),
        scratch_shapes=[pltpu.VMEM(shape, dtype) for shape, dtype in scratch],
        compiler_params=pltpu.CompilerParams(vmem_limit_bytes=limit),
        cost_estimate=pl.CostEstimate(flops=flops, bytes_accessed=size, transcendentals=0),
    )(*args)


def swap(x, axis, size, bit):
    return lax.ppermute(x, axis, [(i, i ^ bit) for i in range(size)])


def gather_xor(x, axis, size):
    blocks = {0: x}
    bit = size // 2
    while bit:
        for j in sorted(blocks):
            if bit > 1:
                blocks[j ^ bit] = swap(blocks[j], axis, size, bit)
        bit //= 2
    parts = []
    for j in range(0, size, 2):
        parts.append(blocks[j])
        count = blocks[j].shape[0] // PIECES
        parts += [
            swap(blocks[j][i * count : (i + 1) * count], axis, size, 1) for i in range(PIECES)
        ]
    return parts


def fold_kernel(root_ref, dinv_ref, after_ref, out_ref):
    rows, depth = root_ref.shape
    block = dinv_ref.shape[0]
    part = block * block // depth
    out_ref[:rows] = root_ref[...]
    for i in range(depth // block):
        out_ref[rows:, i * block : (i + 1) * block] = dinv_ref[i * part : (i + 1) * part]


def after_kernel(value_ref, after_ref, out_ref):
    out_ref[...] = value_ref[...]


def after(value, other):
    return call(after_kernel, [(value.shape, jnp.float32)], [], value, other)[0]


def turn(values, nrow, ncol, block):
    q = ncol // nrow
    out = []
    for t in range(0, ncol, 2):
        pairs = []
        for r in range(nrow):
            for c in range(ncol):
                k = (r * q + c % q) ^ (c // q % 2 * (ncol // 2)) ^ t
                pairs.append(((c // q) * ncol + k, r * ncol + c))
        part = values
        if q > 1:
            which = (lax.axis_index("col") ^ t) % q
            part = lax.dynamic_slice_in_dim(values, which * block, block, 1)
        out.append(lax.ppermute(part, ("row", "col"), pairs))
    return out


def on_device(
    nrow,
    ncol,
    inverse_root,
    lower_first,
    mask_first,
    dinv_first,
    lower_second,
    mask_second,
    parent,
    lower_parent,
    dinv_second,
):
    f32, bf16 = jnp.float32, jnp.bfloat16
    block = dinv_first.shape[0]
    rows, depth = inverse_root.shape
    wide = lower_first.shape
    tiles = mask_first.shape
    cells = lower_first.reshape(tiles[0], BLOCK, tiles[1], BLOCK)
    first = (cells * mask_first.astype(f32)[:, None, :, None]).reshape(wide)
    f_row = [first] + [swap(first, "row", nrow, m) for m in range(nrow - 1, 0, -1)]
    sides = lax.all_gather(lower_parent, "col", axis=0, tiled=True)
    tall = (rows + block * block // depth, depth)
    folded = call(fold_kernel, [(tall, f32)], [], inverse_root, dinv_first, sides)[0]
    r_parts = gather_xor(folded, "col", ncol)
    ordered, child = call(
        functools.partial(child_kernel, nrow, ncol),
        [((ncol * depth, block), f32), (wide, f32)],
        [((ncol, depth, block), f32)],
        *f_row,
        lower_second,
        mask_second.reshape(-1),
        sides,
        parent,
    )
    pair = call(
        pair_kernel, [((2 * depth, wide[1]), f32)], [], child, swap(child, "col", ncol, 1)
    )[0]
    g_parts = turn(pair, nrow, ncol, block)
    f_parts = {0: ordered}
    bit = ncol // 2
    while bit:
        for j in sorted(f_parts):
            here = f_parts[j]
            f_parts[j] = here[: bit * depth]
            sent = here[bit * depth :]
            f_parts[j ^ bit] = swap(after(sent, pair) if 2 * bit == ncol else sent, "col", ncol, bit)
        bit //= 2
    halves = [((ncol, rows, depth), bf16)] * 2
    pieces = [((ncol, depth, 2 * block), bf16)]
    start, r_high, r_low = call(
        functools.partial(panel_kernel, nrow, ncol),
        [((block, block), f32)] + halves,
        [((block, block), f32)],
        *r_parts,
        parent,
        lower_parent,
        dinv_second,
    )
    inverse_first, terms = call(
        functools.partial(first_kernel, nrow, ncol),
        [((rows, block), f32), ((block, block), f32)],
        pieces,
        *[f_parts[j] for j in range(ncol)],
        r_high,
        r_low,
    )
    inverse_second, packed = call(
        functools.partial(second_kernel, nrow, ncol),
        [((rows, block), f32), ((block + 8, block), f32)],
        pieces,
        *g_parts[::-1],
        r_high,
        r_low,
        terms,
    )
    diag_first, diag_second = call(
        last_kernel,
        [((block, block), f32)] * 2,
        [],
        dinv_first,
        start,
        packed,
        *[swap(packed, "row", nrow, j) for j in range(1, nrow)],
    )
    return (inverse_first, diag_first, inverse_second, diag_second)


def solution(mesh):
    in_specs = (
        P(("pole", "row"), "col"),
        P(("pole", "col"), "row"),
        P("col", "row"),
        P("pole", "col"),
        P(("pole", "col"), "row"),
        P("col", "row"),
        P(),
        P("pole", "col"),
        P("pole", "col"),
    )
    out_specs = (
        P(("pole", "row"), "col"),
        P("pole", "col"),
        P(("pole", "row"), "col"),
        P("pole", "col"),
    )
    return jax.shard_map(
        functools.partial(on_device, mesh.shape["row"], mesh.shape["col"]),
        mesh=mesh,
        in_specs=in_specs,
        out_specs=out_specs,
        check_vma=False,
    )
```

```python
import functools

import jax
import jax.numpy as jnp
from jax import lax
from jax.experimental import pallas as pl
from jax.experimental.pallas import tpu as pltpu
from jax.sharding import PartitionSpec as P

VMEM = pl.BlockSpec(memory_space=pltpu.VMEM)
SMEM = pl.BlockSpec(memory_space=pltpu.SMEM)
NN = ((1,), (0,))
TN = ((0,), (0,))
BLOCK = 128
PIECES = 2


def split(x):
    high = x.astype(jnp.bfloat16)
    return high, (x - high.astype(jnp.float32)).astype(jnp.bfloat16)


def dot_split(a, b, dims):
    def one(left, right):
        return lax.dot_general(left, right, (dims, ((), ())), preferred_element_type=jnp.float32)

    return one(a[0], b[0]) + (one(a[0], b[1]) + one(a[1], b[0]))


def dot3(a, b, dims=NN):
    return dot_split(split(a), split(b), dims)


def slots(nrow, ncol):
    q = ncol // nrow
    r, c = lax.axis_index("row"), lax.axis_index("col")
    own = [(r * q + i) ^ c for i in range(q)]
    return (r * q + c % q) ^ (c // q % 2 * (ncol // 2)) ^ c, own, c


def apply_mask(values_ref, pattern_ref, out_ref):
    high, width = values_ref.shape
    across = width // BLOCK
    for i in range(high // BLOCK):
        rows = slice(i * BLOCK, (i + 1) * BLOCK)
        for j in range(across):
            cols = slice(j * BLOCK, (j + 1) * BLOCK)
            factor = pattern_ref[i * across + j].astype(jnp.float32)
            out_ref[rows, cols] = values_ref[rows, cols] * factor


def child_kernel(nrow, ncol, *refs):
    f_refs = refs[:nrow]
    second_ref, pattern_ref, side_ref, parent_ref, sorted_ref, child_ref, held_ref = refs[nrow:]
    q = ncol // nrow
    depth = second_ref.shape[0]
    block = child_ref.shape[1] // q
    r, c = lax.axis_index("row"), lax.axis_index("col")
    for m in range(nrow):
        for j in range(q):
            held_ref[(nrow - m) % nrow * q + j] = f_refs[m][:, j * block : (j + 1) * block]
    for j in range(ncol):
        target = c ^ j
        sorted_ref[j * depth : (j + 1) * depth] = held_ref[((target // q) ^ r) * q + target % q]
    apply_mask(second_ref, pattern_ref, child_ref)
    for j in range(q):
        mine = r * q + j
        above = parent_ref[mine]
        factor = held_ref[((above // q) ^ r) * q + above % q]
        lower = side_ref[pl.ds(pl.multiple_of(mine * block, block), block)]
        cols = slice(j * block, (j + 1) * block)
        child_ref[:, cols] -= dot3(factor, lower)


def pair_kernel(own_ref, other_ref, out_ref):
    depth = own_ref.shape[0]
    out_ref[:depth] = own_ref[...]
    out_ref[depth:] = other_ref[...]


def panel_kernel(nrow, ncol, *refs):
    count = ncol // 2 * (1 + PIECES)
    r_refs = refs[:count]
    parent_ref, lower_ref, dinv_ref, e_ref, rh_ref, rl_ref, sel_ref = refs[count:]
    _, rows, depth = rh_ref.shape
    block = dinv_ref.shape[0]
    part = block * block // depth
    c = lax.axis_index("col")
    chosen = parent_ref[c] ^ c
    for j in range(ncol):
        first = j // 2 * (1 + PIECES)
        here = r_refs[first + 1 : first + 1 + PIECES] if j % 2 else r_refs[first : first + 1]
        start = 0
        for ref in here:
            stop = min(start + ref.shape[0], rows)
            if start < stop:
                rh_ref[j, start:stop], rl_ref[j, start:stop] = split(ref[: stop - start])
            start = stop

        @pl.when(chosen == j)
        def _(last=here[-1]):
            for i in range(depth // block):
                sel_ref[i * part : (i + 1) * part] = last[-part:, i * block : (i + 1) * block]

    lower = split(lower_ref[...])
    product = dot_split(split(sel_ref[...]), lower, NN)
    e_ref[...] = dinv_ref[...] + dot_split(lower, split(product), TN)


def spread(nrow, ncol, refs, w_ref):
    base, own, _ = slots(nrow, ncol)
    depth = refs[0].shape[0] // 2
    block = w_ref.shape[2] // 2
    for t in range(ncol):
        slot = base ^ t
        part = refs[-1 - t // 2][t % 2 * depth : (t % 2 + 1) * depth]
        w_ref[slot, :, :block], w_ref[slot, :, block:] = split(part)
    return own, depth


def products(nrow, ncol, own, depth, r_refs, w_ref):
    block = w_ref.shape[2] // 2

    def one(left, right, dims):
        return lax.dot_general(left, right, (dims, ((), ())), preferred_element_type=jnp.float32)

    wide, rest = None, None
    for j in range(ncol):
        term = one(r_refs[0][j], w_ref[j], NN)
        wide = term if wide is None else wide + term
        term = one(r_refs[1][j], w_ref[j, :, :block], NN)
        rest = term if rest is None else rest + term
    total = wide[:, :block] + (wide[:, block:] + rest)
    diag = None
    for i, slot in enumerate(own):
        high, low = split(total[i * depth : (i + 1) * depth])
        tall = one(w_ref[slot], high, TN)
        term = tall[:block] + (tall[block:] + one(w_ref[slot, :, :block], low, TN))
        diag = term if diag is None else diag + term
    return total, diag


def first_kernel(nrow, ncol, *refs):
    rh_ref, rl_ref, x_ref, d_ref, w_ref = refs[ncol:]
    block = x_ref.shape[1]
    own = slots(nrow, ncol)[1]
    depth = refs[0].shape[0]
    for j in range(ncol):
        w_ref[j, :, :block], w_ref[j, :, block:] = split(refs[j][...])
    total, diag = products(nrow, ncol, own, depth, (rh_ref, rl_ref), w_ref)
    x_ref[...] = -total
    d_ref[...] = diag


def second_kernel(nrow, ncol, *refs):
    rh_ref, rl_ref, d_ref, y_ref, m_ref, w_ref = refs[ncol // 2 :]
    own, depth = spread(nrow, ncol, refs[: ncol // 2], w_ref)
    total, diag = products(nrow, ncol, own, depth, (rh_ref, rl_ref), w_ref)
    y_ref[...] = -total
    block = diag.shape[0]
    across = lax.broadcasted_iota(jnp.int32, diag.shape, 1)
    down = lax.broadcasted_iota(jnp.int32, diag.shape, 0)
    m_ref[:block] = jnp.where(down <= across, d_ref[...], diag)
    line = jnp.sum(jnp.where(down == across, diag, 0.0), axis=0, keepdims=True)
    m_ref[block:] = jnp.broadcast_to(line, (m_ref.shape[0] - block, line.shape[1]))


def last_kernel(dinv_ref, e_ref, *refs):
    one_ref, two_ref = refs[-2:]
    block = dinv_ref.shape[0]
    total = refs[0][...]
    for ref in refs[1:-2]:
        total += ref[...]
    m = total[:block]
    across = lax.broadcasted_iota(jnp.int32, m.shape, 1)
    down = lax.broadcasted_iota(jnp.int32, m.shape, 0)
    turned = m.T
    one_ref[...] = dinv_ref[...] + jnp.where(down <= across, m, turned)
    line = jnp.broadcast_to(total[block : block + 1], m.shape)
    two_ref[...] = e_ref[...] + jnp.where(
        down == across, line, jnp.where(down > across, m, turned)
    )


def call(kernel, outs, scratch, *args, flops=0):
    size = 0
    for shape, dtype in [(a.shape, a.dtype) for a in args] + outs + scratch:
        if len(shape) > 1:
            count = 1
            for extent in shape:
                count *= extent
            size += count * jnp.dtype(dtype).itemsize
    limit = min(56 << 20, 3 * size + (4 << 20))
    return pl.pallas_call(
        kernel,
        out_shape=[jax.ShapeDtypeStruct(shape, dtype) for shape, dtype in outs],
        in_specs=[SMEM if a.ndim == 1 else VMEM for a in args],
        out_specs=[VMEM] * len(outs),
        scratch_shapes=[pltpu.VMEM(shape, dtype) for shape, dtype in scratch],
        compiler_params=pltpu.CompilerParams(vmem_limit_bytes=limit),
        cost_estimate=pl.CostEstimate(flops=flops, bytes_accessed=size, transcendentals=0),
    )(*args)


def swap(x, axis, size, bit):
    return lax.ppermute(x, axis, [(i, i ^ bit) for i in range(size)])


def gather_xor(x, axis, size):
    blocks = {0: x}
    bit = size // 2
    while bit:
        for j in sorted(blocks):
            if bit > 1:
                blocks[j ^ bit] = swap(blocks[j], axis, size, bit)
        bit //= 2
    parts = []
    for j in range(0, size, 2):
        parts.append(blocks[j])
        count = blocks[j].shape[0] // PIECES
        parts += [
            swap(blocks[j][i * count : (i + 1) * count], axis, size, 1) for i in range(PIECES)
        ]
    return parts


def fold_kernel(root_ref, dinv_ref, after_ref, out_ref):
    rows, depth = root_ref.shape
    block = dinv_ref.shape[0]
    part = block * block // depth
    out_ref[:rows] = root_ref[...]
    for i in range(depth // block):
        out_ref[rows:, i * block : (i + 1) * block] = dinv_ref[i * part : (i + 1) * part]


def after_kernel(value_ref, after_ref, out_ref):
    out_ref[...] = value_ref[...]


def after(value, other):
    return call(after_kernel, [(value.shape, jnp.float32)], [], value, other)[0]


def turn(values, nrow, ncol, block):
    q = ncol // nrow
    out = []
    for t in range(0, ncol, 2):
        pairs = []
        for r in range(nrow):
            for c in range(ncol):
                k = (r * q + c % q) ^ (c // q % 2 * (ncol // 2)) ^ t
                pairs.append(((c // q) * ncol + k, r * ncol + c))
        part = values
        if q > 1:
            which = (lax.axis_index("col") ^ t) % q
            part = lax.dynamic_slice_in_dim(values, which * block, block, 1)
        out.append(lax.ppermute(part, ("row", "col"), pairs))
    return out


def on_device(
    nrow,
    ncol,
    inverse_root,
    lower_first,
    mask_first,
    dinv_first,
    lower_second,
    mask_second,
    parent,
    lower_parent,
    dinv_second,
):
    f32, bf16 = jnp.float32, jnp.bfloat16
    block = dinv_first.shape[0]
    rows, depth = inverse_root.shape
    wide = lower_first.shape
    tiles = mask_first.shape
    cells = lower_first.reshape(tiles[0], BLOCK, tiles[1], BLOCK)
    first = (cells * mask_first.astype(f32)[:, None, :, None]).reshape(wide)
    f_row = [first] + [swap(first, "row", nrow, m) for m in range(nrow - 1, 0, -1)]
    sides = lax.all_gather(lower_parent, "col", axis=0, tiled=True)
    tall = (rows + block * block // depth, depth)
    folded = call(fold_kernel, [(tall, f32)], [], inverse_root, dinv_first, sides)[0]
    r_parts = gather_xor(folded, "col", ncol)
    ordered, child = call(
        functools.partial(child_kernel, nrow, ncol),
        [((ncol * depth, block), f32), (wide, f32)],
        [((ncol, depth, block), f32)],
        *f_row,
        lower_second,
        mask_second.reshape(-1),
        sides,
        parent,
    )
    pair = call(
        pair_kernel, [((2 * depth, wide[1]), f32)], [], child, swap(child, "col", ncol, 1)
    )[0]
    g_parts = turn(pair, nrow, ncol, block)
    f_parts = {0: ordered}
    bit = ncol // 2
    while bit:
        for j in sorted(f_parts):
            here = f_parts[j]
            f_parts[j] = here[: bit * depth]
            sent = here[bit * depth :]
            f_parts[j ^ bit] = swap(after(sent, pair) if 2 * bit == ncol else sent, "col", ncol, bit)
        bit //= 2
    halves = [((ncol, rows, depth), bf16)] * 2
    pieces = [((ncol, depth, 2 * block), bf16)]
    start, r_high, r_low = call(
        functools.partial(panel_kernel, nrow, ncol),
        [((block, block), f32)] + halves,
        [((block, block), f32)],
        *r_parts,
        parent,
        lower_parent,
        dinv_second,
    )
    inverse_first, terms = call(
        functools.partial(first_kernel, nrow, ncol),
        [((rows, block), f32), ((block, block), f32)],
        pieces,
        *[f_parts[j] for j in range(ncol)],
        r_high,
        r_low,
    )
    inverse_second, packed = call(
        functools.partial(second_kernel, nrow, ncol),
        [((rows, block), f32), ((block + 8, block), f32)],
        pieces,
        *g_parts[::-1],
        r_high,
        r_low,
        terms,
    )
    diag_first, diag_second = call(
        last_kernel,
        [((block, block), f32)] * 2,
        [],
        dinv_first,
        start,
        packed,
        *[swap(packed, "row", nrow, j) for j in range(nrow - 1, 0, -1)],
    )
    return (inverse_first, diag_first, inverse_second, diag_second)


def solution(mesh):
    in_specs = (
        P(("pole", "row"), "col"),
        P(("pole", "col"), "row"),
        P("col", "row"),
        P("pole", "col"),
        P(("pole", "col"), "row"),
        P("col", "row"),
        P(),
        P("pole", "col"),
        P("pole", "col"),
    )
    out_specs = (
        P(("pole", "row"), "col"),
        P("pole", "col"),
        P(("pole", "row"), "col"),
        P("pole", "col"),
    )
    return jax.shard_map(
        functools.partial(on_device, mesh.shape["row"], mesh.shape["col"]),
        mesh=mesh,
        in_specs=in_specs,
        out_specs=out_specs,
        check_vma=False,
    )
```
